512 devices in a mesh: sta: 128 (over z, y, core), sec: 4 (over x).
Axes of the slice: x: 4, y: 4, z: 16, core: 2. Of those that a mesh axis runs over, the one named last changes fastest.
Arguments:
- raw_traces: bfloat16 [49152, 4096], P('sta', 'sec'), may hold values from -1200 to 1200
- fir_taps: float32 [33], replicated, may hold values from -1 to 1
- tile_pairs: int32 [16384, 2], replicated, may hold values from 0 to 4095, as said below
- tile_count: int32 [16384], P('sta'), may hold values from 0 to 4
Outputs:
- coherency: float32 [16, 2, 12, 196608], P('sec', None, None, 'sta')
The draws below stay inside these ranges and needn't reach their ends.
Inputs may be any that keep to these rules, and one draw needn't show every extreme that they name: `tile_pairs`: tile t belongs to owner t // 128 along sta. Device u along sta holds blocks u * 32 to (u + 1) * 32 - 1. Among the 256 block ids of one owner's tiles, exactly two are held by each device u, and those two are equal.
All inputs are finite; a program needn't handle non-finite values.
Results may differ from the reference program's by a relative error of at most 0.004.
Values may be sent and summed in bfloat16 or wider, within the bound.
A program may use at most 128 MiB of HBM per device.

```python
import math
import jax
import jax.numpy as jnp
from jax import lax

SPD = 128
SBK = 4
L = 4096
F = 1024
LOWBIN = 4
WB = 64
FH = 16
NH = 32
BR = 12
BPD = 32
NBLK = 4096
TPD = 128
TILES = 16384
ROWS = 49152
NBAND = 16
N_STA = 128


def draw_raw_traces(key, part):
    key = jax.random.fold_in(key, 5)
    key_values, key_rows, key_envelope = jax.random.split(key, 3)
    values = jnp.clip(jax.random.normal(key_values, (ROWS, L), jnp.float32), -4.0, 4.0)
    row_top = 10.0
    row_scale = jnp.exp(jax.random.uniform(key_rows, (ROWS, 1), jnp.float32, 0.0, math.log(row_top)))
    envelope = jnp.exp(jax.random.uniform(key_envelope, (ROWS, L // 64), jnp.float32, 0.0, math.log(10.0)))
    return (values * row_scale * jnp.repeat(envelope, 64, axis=1)).astype(jnp.bfloat16)


def draw_tile_pairs(key, part):
    key = jax.random.fold_in(key, 9)
    key_local, key_top, key_low, key_order = jax.random.split(key, 4)
    local_pick = jax.random.randint(key_local, (TPD, TPD), 0, BPD)
    top_owner = jax.random.randint(key_top, (), 0, TPD)
    low_owner = jax.random.randint(key_low, (), 0, TPD)
    local_pick = local_pick.at[top_owner, TPD - 1].set(BPD - 1)
    local_pick = local_pick.at[low_owner, 0].set(0)
    blocks = jnp.arange(TPD, dtype=jnp.int32)[None, :] * BPD + local_pick
    doubled = jnp.repeat(blocks, 2, axis=1)
    orders = jax.vmap(lambda subkey: jax.random.permutation(subkey, 2 * TPD))(jax.random.split(key_order, TPD))
    end_list = jnp.take_along_axis(doubled, orders, axis=1)
    return end_list.reshape(TPD * TPD, 2).astype(jnp.int32)


def plant(values, stream_key, smallest, largest):
    dims = values.shape
    spot = [jax.random.randint(jax.random.fold_in(stream_key, axis), (), 0, dims[axis]) for axis in range(len(dims))]
    values = values.at[tuple(spot)].set(smallest)
    longest = dims.index(max(dims))
    spot[longest] = (spot[longest] + 1) % dims[longest]
    return values.at[tuple(spot)].set(largest)


def scatter_about(rng, extent, width, reach, kind=jnp.bfloat16):
    return jnp.clip(width * jax.random.normal(rng, extent, jnp.float32), -reach, reach).astype(kind)


def setup_inputs(seed: int = 0) -> dict:
    key_list = jax.random.split(jax.random.key(seed), 5)
    return {
        "raw_traces": draw_raw_traces(jax.random.fold_in(key_list[4], 71), 0),
        "fir_taps": scatter_about(key_list[1], (2 * FH + 1,), (2 * FH + 1) ** -0.5, 1.0, jnp.float32),
        "tile_pairs": draw_tile_pairs(jax.random.fold_in(key_list[4], 71), 0),
        "tile_count": plant(jax.random.randint(key_list[3], (TILES,), 0, SBK + 1), jax.random.fold_in(key_list[3], 1), 0, SBK).astype(jnp.int32),
    }


def prepare(group_raw, fir_taps):
    signal_ext = jnp.pad(group_raw.astype(jnp.float32), ((0, 0), (FH + NH, FH + NH)))
    filtered = lax.conv_general_dilated(signal_ext[:, None, :], fir_taps[None, None, :], (1,), 'VALID', precision=lax.Precision.HIGHEST)[:, 0, :]
    mean_level = lax.reduce_window(jnp.abs(filtered), jnp.zeros((), filtered.dtype), lax.add, (1, 2 * NH + 1), (1, 1), 'VALID') / (2 * NH + 1)
    normed = filtered[:, NH:NH + L] / (mean_level + 1e-05)
    spectrum = jnp.fft.rfft(normed, axis=1)[:, LOWBIN:LOWBIN + F]
    real_part = jnp.real(spectrum)
    imag_part = jnp.imag(spectrum)
    band_power = lax.optimization_barrier(jnp.mean((real_part * real_part + imag_part * imag_part).reshape(-1, NBAND, WB), axis=2))
    scale_norm = jnp.sqrt(band_power + 1e-06)[:, :, None]
    real_white = (real_part.reshape(-1, NBAND, WB) / scale_norm).reshape(-1, F).astype(jnp.bfloat16)
    imag_white = (imag_part.reshape(-1, NBAND, WB) / scale_norm).reshape(-1, F).astype(jnp.bfloat16)
    return (real_white, imag_white)

def reference(raw_traces, fir_taps, tile_pairs, tile_count):
    group_rows = 3 * SPD
    groups = raw_traces.reshape(N_STA, group_rows, L)
    real_white, imag_white = lax.map(lambda group_raw: prepare(group_raw, fir_taps), groups)
    real_blocks = real_white.reshape(NBLK, BR, F)
    imag_blocks = imag_white.reshape(NBLK, BR, F)
    pair_groups = tile_pairs.reshape(N_STA, TPD, 2)
    count_groups = tile_count.reshape(N_STA, TPD)

    def owner_tiles(inputs):
        owner_pairs, owner_counts = inputs

        def fetch_side(source_table, column):
            return source_table[owner_pairs[:, column]].astype(jnp.float32).reshape(TPD, BR, NBAND, WB)
        left_real = fetch_side(real_blocks, 0)
        left_imag = fetch_side(imag_blocks, 0)
        right_real = fetch_side(real_blocks, 1)
        right_imag = fetch_side(imag_blocks, 1)
        pattern = 'sibf,sjbf->bisj'
        real_sum = jnp.einsum(pattern, left_real, right_real) + jnp.einsum(pattern, left_imag, right_imag)
        imag_sum = jnp.einsum(pattern, left_imag, right_real) - jnp.einsum(pattern, left_real, right_imag)
        valid_mask = jnp.arange(BR, dtype=jnp.int32)[None, :] // 3 < owner_counts[:, None]
        return jnp.stack([real_sum, imag_sum], axis=1) * (1.0 / WB) * valid_mask[None, None, None]
    stacked = lax.map(owner_tiles, (pair_groups, count_groups))
    return jnp.transpose(stacked, (1, 2, 3, 0, 4, 5)).reshape(NBAND, 2, BR, TILES * BR)
```

```python
import functools
import math

import jax
import jax.numpy as jnp
import numpy as np
from jax import lax
from jax.experimental import pallas as pl
from jax.experimental.pallas import tpu as pltpu
from jax.sharding import PartitionSpec as P

MESH = pl.DeviceIdType.MESH
L = 4096
F = 1024
LOWBIN = 4
WB = 64
FH = 16
NH = 32
BR = 12
PLANE = 8
NZ = 16
NX = 4
REACH = 4
CROWS = 48
BLK = 4 * BR
F32 = jnp.float32
BF16 = jnp.bfloat16


def dft_tables():
    cols = np.arange(512)
    sect, part, band, mm = cols // 128, (cols // 64) % 2, (cols // 16) % 4, cols % 16
    m = (4 * sect + band) * 16 + mm + 1
    t = np.arange(1024)
    planes = []
    for r in (0, 2, 1, 3):
        angle = 2.0 * np.pi / L * ((t[:, None] * (4 * m + r)[None, :]) % L)
        planes.append(np.where(part[None, :] == 0, np.cos(angle), -np.sin(angle)))
    return np.concatenate(planes).astype(np.float32)


def split(value):
    high = value.astype(BF16)
    return high, (value - high.astype(F32)).astype(BF16)


def mm(a, b):
    return jnp.dot(a, b, preferred_element_type=F32)


def build_filters(taps_ref, toep_ref, box_ref):
    def rows(i, carry):
        start = pl.multiple_of(32 * i, 32)
        diff = (
            lax.broadcasted_iota(jnp.int32, (32, 256), 0)
            + 32 * i
            - lax.broadcasted_iota(jnp.int32, (32, 256), 1)
        )
        first = jnp.zeros((32, 256), F32)
        second = jnp.zeros((32, 256), F32)
        for k in range(2 * FH + 1):
            tap = taps_ref[k]
            first = jnp.where(diff == k + 112, tap, first)
            second = jnp.where(diff == k - 144, tap, second)
        for which, value in enumerate((first, second)):
            high, low = split(value)
            toep_ref[which, 0, pl.ds(start, 32)] = high
            toep_ref[which, 1, pl.ds(start, 32)] = low
        box_ref[0, pl.ds(start, 32)] = jnp.where(jnp.abs(diff - 128) <= NH, 1.0, 0.0).astype(BF16)
        box_ref[1, pl.ds(start, 32)] = jnp.where(jnp.abs(diff + 128) <= NH, 1.0, 0.0).astype(BF16)
        return carry

    lax.fori_loop(0, 8, rows, 0)


def split_tables(wide, tab_ref):
    def rows(i, carry):
        start = pl.multiple_of(32 * i, 32)
        for r in range(4):
            high, low = split(wide[pl.ds(1024 * r + start, 32)])
            tab_ref[0, r, pl.ds(start, 32)] = high
            tab_ref[1, r, pl.ds(start, 32)] = low
        return carry

    lax.fori_loop(0, 32, rows, 0)


def normalize(xin, toep_ref, box_ref, filt, mag):
    n = CROWS
    x0 = xin[0:17].reshape(17 * n, 256)
    x1 = xin[1:18].reshape(17 * n, 256)
    filtered = (mm(x0, toep_ref[0, 0]) + mm(x1, toep_ref[1, 0])) + (
        mm(x0, toep_ref[0, 1]) + mm(x1, toep_ref[1, 1])
    )
    filt[...] = filtered.reshape(17, n, 256)
    high, low = split(jnp.abs(filtered))
    mag[0] = high.reshape(17, n, 256)
    mag[1] = low.reshape(17, n, 256)
    level = (
        mm(mag[0, 0:16].reshape(16 * n, 256), box_ref[0])
        + mm(mag[0, 1:17].reshape(16 * n, 256), box_ref[1])
    ) + (
        mm(mag[1, 0:16].reshape(16 * n, 256), box_ref[0])
        + mm(mag[1, 1:17].reshape(16 * n, 256), box_ref[1])
    )
    center = jnp.concatenate([filt[0:16, :, 128:256], filt[1:17, :, 0:128]], axis=-1)
    return center / (level.reshape(16, n, 256) * (1.0 / (2 * NH + 1)) + 1e-05)


def spectra_of(normed, tab_ref):
    n = CROWS
    seg = normed.reshape(4, 4, n, 256)
    even, odd = seg[0] + seg[2], seg[1] + seg[3]
    flat = lambda v: jnp.concatenate([v[k] for k in range(4)], axis=-1)
    y0, y2 = flat(even + odd), flat(even - odd)
    ya, yb = flat(seg[0] - seg[2]), flat(seg[1] - seg[3])

    def transform(value, r):
        rows = value.shape[0]
        high, low = split(value)
        both = mm(jnp.concatenate([high, low], axis=0), tab_ref[0, r])
        return both[:rows] + both[rows:] + mm(high, tab_ref[1, r])

    s0 = transform(y0, 0)
    s2 = transform(y2, 1)
    ab = jnp.concatenate([ya, yb], axis=0)
    odd1, odd3 = transform(ab, 2), transform(ab, 3)
    lane = lax.broadcasted_iota(jnp.int32, (n, 512), 1)
    sign = jnp.where((lane // 64) % 2 == 0, 1.0, -1.0)

    def swap(value):
        return jnp.concatenate(
            [pltpu.roll(value[:, 128 * s : 128 * s + 128], 64, 1) for s in range(4)], axis=-1
        )

    s1 = odd1[:n] + sign * swap(odd1[n:])
    s3 = odd3[:n] - sign * swap(odd3[n:])
    return s0, s1, s2, s3


def whiten(spectra, stage, out_ref):
    n = CROWS
    power = sum(s * s for s in spectra)
    li = lax.broadcasted_iota(jnp.int32, (128, 128), 0)
    lj = lax.broadcasted_iota(jnp.int32, (128, 128), 1)
    group = jnp.where((li // 16) % 4 == (lj // 16) % 4, 1.0, 0.0).astype(BF16)
    tall = jnp.concatenate([power[:, 128 * s : 128 * s + 128] for s in range(4)], axis=0)
    high, low = split(tall)
    band = mm(high, group) + mm(low, group)
    scale = lax.rsqrt(band * (1.0 / WB) + 1e-06)
    slot = (lax.broadcasted_iota(jnp.int32, (n, 128), 1) // 16) % 4
    for s in range(4):
        sc = scale[n * s : n * s + n]
        parts = [spectra[r][:, 128 * s : 128 * s + 128] * sc for r in range(4)]
        for b in range(4):
            value = None
            for r in range(4):
                moved = parts[r] if r == b else pltpu.roll(parts[r], (16 * (r - b)) % 128, 1)
                value = moved if value is None else jnp.where(slot == r, moved, value)
            for k in range(4):
                stage[s, BLK * k + BR * b : BLK * k + BR * b + BR, :] = value[BR * k : BR * k + BR]
        out_ref[s] = stage[s].astype(BF16).reshape(4, BLK, 128)


def exchange_kernel(
    raw_ref, taps_ref, ends_ref, tab_hbm, out_ref,
    wide, tab, xin, toep, box, filt, mag, stage, wsend, pick_v, pick_s,
    near_stage, far_stage,
    slot0, slot1, slot2, slot3, slot4, slot5, slot6, slot7, slot8,
    tab_sem, own_sem, xs_sem, xr_sem, bs_sem, br_sem, zs_sem, zr_sem,
    ps_sem, pr_sem, loc_sem, pk_sem,
):
    slots = (slot0, slot1, slot2, slot3, slot4, slot5, slot6, slot7, slot8)
    sta = lax.axis_index("sta")
    x = lax.axis_index("sec")
    z = sta // PLANE
    w = sta % PLANE
    core = sta % 2

    def plane(step):
        return (z + step + NZ) % NZ

    def at(step, ww):
        return plane(step) * PLANE + ww

    def xpeer(i):
        return (x + i) % NX

    barrier = pltpu.get_barrier_semaphore()

    def greet(step, ww):
        pl.semaphore_signal(barrier, inc=1, device_id=(at(step, ww), x), device_id_type=MESH)

    for i in range(1, NX):
        pl.semaphore_signal(barrier, inc=1, device_id=(sta, xpeer(i)), device_id_type=MESH)

    def greet_plane(i, carry):
        for step in (1, 2, 3, -1, -2, -3):
            greet(step, i)
        return carry

    lax.fori_loop(0, PLANE, greet_plane, 0)

    def greet_own(i, carry):
        greet(0, (w + i) % PLANE)
        return carry

    lax.fori_loop(1, PLANE, greet_own, 0)
    antipode = jnp.where(core == 0, -REACH, REACH)

    def greet_far(i, carry):
        greet(antipode, i)
        return carry

    lax.fori_loop(0, PLANE, greet_far, 0)

    tab_copy = pltpu.make_async_copy(tab_hbm, wide, tab_sem)
    tab_copy.start()

    def own_copy(c, k):
        return pltpu.make_async_copy(
            raw_ref.at[pl.ds(pl.multiple_of(96 * x + CROWS * c, 16), CROWS), 256 * k : 256 * k + 256],
            xin.at[c, 1 + 4 * x + k],
            own_sem.at[c, k],
        )

    for c in range(2):
        for k in range(4):
            own_copy(c, k).start()

    pl.semaphore_wait(barrier, 3 + 7 + 48 + 8)

    def raw_copy(c, i, k):
        return pltpu.make_async_remote_copy(
            src_ref=raw_ref.at[
                pl.ds(pl.multiple_of(96 * xpeer(i) + CROWS * c, 16), CROWS), 256 * k : 256 * k + 256
            ],
            dst_ref=xin.at[c, 1 + 4 * x + k],
            send_sem=xs_sem.at[c, i - 1, k],
            recv_sem=xr_sem.at[c, i - 1, k],
            device_id=(sta, xpeer(i)),
            device_id_type=MESH,
        )

    for c in range(2):
        for i in (2, 1, 3):
            for k in range(4):
                raw_copy(c, i, k).start()

    zero = jnp.zeros((CROWS, 256), BF16)
    for c in range(2):
        xin[c, 0] = zero
        xin[c, 17] = zero
    build_filters(taps_ref, toep, box)
    lane = lax.broadcasted_iota(jnp.int32, (16, 128), 1)
    picks = jnp.zeros((16, 128), jnp.int32)

    def asked(step, source):
        rows = ends_ref[pl.ds(pl.multiple_of(16 * plane(step), 16), 16), :]
        return jnp.max(jnp.where(rows // 32 == source, rows % 32, 0), axis=1, keepdims=True)

    wanted = [(0, at(-s if s <= REACH else s - REACH, w)) for s in range(9)]
    wanted += [(h, at(-REACH, w)) for h in range(1, REACH + 1)]
    wanted += [(-h, at(REACH, w)) for h in range(1, REACH + 1)]
    for col, (step, source) in enumerate(wanted):
        picks = jnp.where(lane == col, asked(step, source), picks)
    pick_v[...] = picks
    pick_copy = pltpu.make_async_copy(pick_v, pick_s, pk_sem)
    pick_copy.start()
    tab_copy.wait()
    split_tables(wide, tab)
    pick_copy.wait()

    def back_copy(c, i):
        rows = pl.ds(8 * x + 4 * c, 4)
        return pltpu.make_async_remote_copy(
            src_ref=wsend.at[c, xpeer(i)],
            dst_ref=slot0.at[rows],
            send_sem=bs_sem.at[c, i - 1],
            recv_sem=br_sem.at[c, i - 1],
            device_id=(sta, xpeer(i)),
            device_id_type=MESH,
        )

    def back_wait(c, i):
        rows = pl.ds(8 * ((x + NX - i) % NX) + 4 * c, 4)
        pltpu.make_async_copy(slot0.at[rows], slot0.at[rows], br_sem.at[c, i - 1]).wait()

    def ring_copy(d, h, c, i):
        rows = pl.ds(8 * ((x + NX - i) % NX) + 4 * c, 4)
        source = slot0 if h == 1 else slots[h - 1 + 4 * d]
        return pltpu.make_async_remote_copy(
            src_ref=source.at[rows],
            dst_ref=slots[h + 4 * d].at[rows],
            send_sem=zs_sem.at[d, h - 1, 4 * c + i],
            recv_sem=zr_sem.at[d, h - 1, 4 * c + i],
            device_id=(at(1 - 2 * d, w), x),
            device_id_type=MESH,
        )

    def ring_start(h, c, i):
        for d in range(2):
            if h > 1:
                ring_copy(d, h - 1, c, i).wait_recv()
            ring_copy(d, h, c, i).start()

    def raw_wait(c):
        for k in range(4):
            own_copy(c, k).wait()
        for i in range(1, NX):
            for k in range(4):
                dst = xin.at[c, 1 + 4 * ((x + NX - i) % NX) + k]
                pltpu.make_async_copy(dst, dst, xr_sem.at[c, i - 1, k]).wait()

    def back_start(c):
        slot0[pl.ds(8 * x + 4 * c, 4)] = wsend[c, x]
        ring_start(1, c, 0)
        for i in (2, 1, 3):
            back_copy(c, i).start()

    def asked_block(ww, col):
        return jnp.clip(jnp.maximum(pick_s[2 * ww, col], pick_s[2 * ww + 1, col]), 0, 31)

    def near_picks(s):
        def one(i, carry):
            ww = (w + i) % PLANE
            near_stage[s, i] = slots[s][asked_block(ww, s)]
            return carry

        lax.fori_loop(0, PLANE, one, 0)
        source = at(-s if s <= REACH else s - REACH, w)

        def send(i, carry):
            pltpu.make_async_remote_copy(
                src_ref=near_stage.at[s, i],
                dst_ref=out_ref.at[source],
                send_sem=ps_sem,
                recv_sem=pr_sem,
                device_id=(at(0, (w + i) % PLANE), x),
                device_id_type=MESH,
            ).start()
            return carry

        lax.fori_loop(1, PLANE, send, 0)
        pltpu.make_async_copy(near_stage.at[s, 0], out_ref.at[source], loc_sem.at[s]).start()

    def far_picks(d):
        s = REACH + 4 * d
        sign = 1 - 2 * d
        source = at(-REACH * sign, w)

        def send(row, h, ww):
            pltpu.make_async_remote_copy(
                src_ref=far_stage.at[d, row],
                dst_ref=out_ref.at[source],
                send_sem=ps_sem,
                recv_sem=pr_sem,
                device_id=(at(h * sign, ww), x),
                device_id_type=MESH,
            ).start()

        def grab(row, h, ww):
            col = 9 + 4 * d + h - 1
            far_stage[d, row] = slots[s][asked_block(ww, col)]

        def last(i, carry):
            grab(24 + i, REACH, 2 * i + d)
            send(24 + i, REACH, 2 * i + d)
            return carry

        lax.fori_loop(0, PLANE // 2, last, 0)
        for h in (3, 2, 1):
            def one(i, carry):
                grab(8 * (h - 1) + i, h, i)
                send(8 * (h - 1) + i, h, i)
                return carry

            lax.fori_loop(0, PLANE, one, 0)

    raw_wait(0)
    normed = normalize(xin.at[0], toep, box, filt, mag)
    whiten(spectra_of(normed, tab), stage, wsend.at[0])
    back_start(0)
    raw_wait(1)
    normed = normalize(xin.at[1], toep, box, filt, mag)
    for i in range(1, NX):
        back_wait(0, i)
        ring_start(1, 0, i)
    whiten(spectra_of(normed, tab), stage, wsend.at[1])
    back_start(1)
    for i in range(1, NX):
        back_wait(1, i)
        ring_start(1, 1, i)
    near_picks(0)
    for h in range(2, REACH + 1):
        for c in range(2):
            for i in range(NX):
                ring_start(h, c, i)
        near_picks(h - 1)
        near_picks(h - 1 + 4)
    for c in range(2):
        for i in range(NX):
            for d in range(2):
                ring_copy(d, REACH, c, i).wait_recv()
    far_picks(0)
    far_picks(1)
    near_picks(REACH)
    near_picks(2 * REACH)

    for s in range(9):
        pltpu.make_async_copy(near_stage.at[s, 0], out_ref.at[0], loc_sem.at[s]).wait()
    for c in range(2):
        for i in range(1, NX):
            for k in range(4):
                raw_copy(c, i, k).wait_send()
            back_copy(c, i).wait_send()
        for h in range(1, REACH + 1):
            for i in range(NX):
                for d in range(2):
                    ring_copy(d, h, c, i).wait_send()
    total = out_ref.at[0:119]
    pltpu.make_async_copy(total, total, ps_sem).wait()
    pltpu.make_async_copy(total, total, pr_sem).wait()


def exchange(raw, taps, ends, tab):
    any_spec = pl.BlockSpec(memory_space=pl.ANY)
    slot = pltpu.VMEM((32, BLK, 128), BF16)
    dma = pltpu.SemaphoreType.DMA
    return pl.pallas_call(
        exchange_kernel,
        out_shape=jax.ShapeDtypeStruct((NZ * PLANE, BLK, 128), BF16),
        in_specs=[
            any_spec,
            pl.BlockSpec(memory_space=pltpu.SMEM),
            pl.BlockSpec(memory_space=pltpu.VMEM),
            any_spec,
        ],
        out_specs=any_spec,
        scratch_shapes=[
            pltpu.VMEM((4096, 512), F32),
            pltpu.VMEM((2, 4, 1024, 512), BF16),
            pltpu.VMEM((2, 18, CROWS, 256), BF16),
            pltpu.VMEM((2, 2, 256, 256), BF16),
            pltpu.VMEM((2, 256, 256), BF16),
            pltpu.VMEM((17, CROWS, 256), F32),
            pltpu.VMEM((2, 17, CROWS, 256), BF16),
            pltpu.VMEM((4, 4 * BLK, 128), F32),
            pltpu.VMEM((2, 4, 4, BLK, 128), BF16),
            pltpu.VMEM((16, 128), jnp.int32),
            pltpu.SMEM((16, 128), jnp.int32),
            pltpu.VMEM((9, PLANE, BLK, 128), BF16),
            pltpu.VMEM((2, 28, BLK, 128), BF16),
        ]
        + [slot] * 9
        + [
            dma, dma((2, 4)), dma((2, 3, 4)), dma((2, 3, 4)), dma((2, 3)), dma((2, 3)),
            dma((2, 4, 8)), dma((2, 4, 8)), dma, dma, dma((9,)), dma,
        ],
        compiler_params=pltpu.CompilerParams(
            collective_id=0, has_side_effects=True, vmem_limit_bytes=56 << 20
        ),
        name="exchange",
    )(raw, taps, ends, tab)


def cross_kernel(ends_hbm, got_ref, count_ref, mask_ref, col_ref, out_ref, ends, left, right, turned, sem):
    sta = lax.axis_index("sta")
    w = sta % PLANE
    copy = pltpu.make_async_copy(
        ends_hbm.at[pl.ds(pl.multiple_of(16 * (sta // PLANE), 16), 16)], ends, sem
    )
    copy.start()
    copy.wait()
    sign = jnp.where(lax.broadcasted_iota(jnp.int32, (BLK, 128), 1) < 64, -1.0, 1.0)

    def gather(g, carry):
        rows = pl.ds(pl.multiple_of(BLK * g, 16), BLK)
        for e in range(2):
            tiles = [got_ref[ends[2 * w + e, 4 * g + k] // 32].astype(F32) for k in range(4)]
            for b in range(4):
                value = jnp.concatenate([t[BR * b : BR * b + BR] for t in tiles], axis=0)
                if e == 0:
                    left[b, rows] = value.astype(BF16)
                else:
                    right[b, rows] = value.astype(BF16)
                    turned[b, rows] = (sign * pltpu.roll(value, 64, 1)).astype(BF16)
        return carry

    lax.fori_loop(0, 32, gather, 0)
    tile = lax.broadcasted_iota(jnp.int32, (128, 1536), 0)
    column = lax.broadcasted_iota(jnp.int32, (128, 1536), 1)
    offset = column - BR * tile
    spread = jnp.where((offset >= 0) & (offset < BR), 1.0, 0.0).astype(BF16)
    counts = jnp.broadcast_to(count_ref[...].astype(F32), (8, 128)).astype(BF16)
    valid = jnp.where(col_ref[...] < mm(counts, spread), 1.0 / WB, 0.0)[0:1]
    for b in range(4):
        for cg in range(12):
            first = 2 * (128 * cg // 24)
            rows = left[b, BR * first : BR * first + 144]
            cols = slice(128 * cg, 128 * cg + 128)
            other = jnp.concatenate([right[b, cols], turned[b, cols]], axis=0)
            full = lax.dot_general(
                rows, other, (((1,), (1,)), ((), ())), preferred_element_type=F32
            )
            total = jnp.zeros((24, 256), F32)
            for k in range(6):
                keep = mask_ref[cg % 3, 24 * k : 24 * k + 24]
                total += jnp.concatenate([keep, keep], axis=1) * full[24 * k : 24 * k + 24]
            short = total[:BR] + total[BR:]
            out_ref[b, 0, :, cols] = short[:, :128] * valid[:, cols]
            out_ref[b, 1, :, cols] = short[:, 128:] * valid[:, cols]


def cross(ends, got, counts):
    vmem = pl.BlockSpec(memory_space=pltpu.VMEM)
    mask = np.zeros((3, 144, 128), np.float32)
    for cg in range(3):
        first = 2 * (128 * cg // 24)
        mask[cg] = (first + np.arange(144) // BR)[:, None] == ((128 * cg + np.arange(128)) // BR)[None, :]
    station = np.broadcast_to((np.arange(1536) % BR // 3).astype(np.float32), (8, 1536))
    return pl.pallas_call(
        cross_kernel,
        out_shape=jax.ShapeDtypeStruct((4, 2, BR, 1536), F32),
        in_specs=[pl.BlockSpec(memory_space=pl.ANY), vmem, vmem, vmem, vmem],
        out_specs=vmem,
        scratch_shapes=[
            pltpu.SMEM((16, 128), jnp.int32),
            pltpu.VMEM((4, 1536, 128), BF16),
            pltpu.VMEM((4, 1536, 128), BF16),
            pltpu.VMEM((4, 1536, 128), BF16),
            pltpu.SemaphoreType.DMA,
        ],
        compiler_params=pltpu.CompilerParams(vmem_limit_bytes=48 << 20),
        name="cross",
    )(ends, got, counts, jnp.asarray(mask), jnp.asarray(station))


def body(raw, taps, pairs, counts):
    ends = pairs.reshape(128, 128, 2).transpose(0, 2, 1).reshape(256, 128)
    got = exchange(raw, taps, ends, jnp.asarray(dft_tables()))
    return cross(ends, got, counts.reshape(1, 128))


def solution(mesh):
    return jax.shard_map(
        body,
        mesh=mesh,
        in_specs=(P("sta", "sec"), P(), P(), P("sta")),
        out_specs=P("sec", None, None, "sta"),
        check_vma=False,
    )
```

```python
import functools
import math

import jax
import jax.numpy as jnp
import numpy as np
from jax import lax
from jax.experimental import pallas as pl
from jax.experimental.pallas import tpu as pltpu
from jax.sharding import PartitionSpec as P

MESH = pl.DeviceIdType.MESH
L = 4096
F = 1024
LOWBIN = 4
WB = 64
FH = 16
NH = 32
BR = 12
PLANE = 8
NZ = 16
NX = 4
REACH = 4
CROWS = 48
BLK = 4 * BR
F32 = jnp.float32
BF16 = jnp.bfloat16


def dft_tables():
    cols = np.arange(512)
    sect, part, band, mm = cols // 128, (cols // 64) % 2, (cols // 16) % 4, cols % 16
    m = (4 * sect + band) * 16 + mm + 1
    t = np.arange(1024)
    planes = []
    for r in (0, 2, 1, 3):
        angle = 2.0 * np.pi / L * ((t[:, None] * (4 * m + r)[None, :]) % L)
        planes.append(np.where(part[None, :] == 0, np.cos(angle), -np.sin(angle)))
    return np.concatenate(planes).astype(np.float32)


def split(value):
    high = value.astype(BF16)
    return high, (value - high.astype(F32)).astype(BF16)


def mm(a, b):
    return jnp.dot(a, b, preferred_element_type=F32)


def build_filters(taps_ref, toep_ref, box_ref):
    def rows(i, carry):
        start = pl.multiple_of(32 * i, 32)
        diff = (
            lax.broadcasted_iota(jnp.int32, (32, 256), 0)
            + 32 * i
            - lax.broadcasted_iota(jnp.int32, (32, 256), 1)
        )
        first = jnp.zeros((32, 256), F32)
        second = jnp.zeros((32, 256), F32)
        for k in range(2 * FH + 1):
            tap = taps_ref[k]
            first = jnp.where(diff == k + 112, tap, first)
            second = jnp.where(diff == k - 144, tap, second)
        for which, value in enumerate((first, second)):
            high, low = split(value)
            toep_ref[which, 0, pl.ds(start, 32)] = high
            toep_ref[which, 1, pl.ds(start, 32)] = low
        box_ref[0, pl.ds(start, 32)] = jnp.where(jnp.abs(diff - 128) <= NH, 1.0, 0.0).astype(BF16)
        box_ref[1, pl.ds(start, 32)] = jnp.where(jnp.abs(diff + 128) <= NH, 1.0, 0.0).astype(BF16)
        return carry

    lax.fori_loop(0, 8, rows, 0)


def split_tables(wide, tab_ref):
    def rows(i, carry):
        start = pl.multiple_of(32 * i, 32)
        for r in range(4):
            high, low = split(wide[pl.ds(1024 * r + start, 32)])
            tab_ref[0, r, pl.ds(start, 32)] = high
            tab_ref[1, r, pl.ds(start, 32)] = low
        return carry

    lax.fori_loop(0, 32, rows, 0)


def normalize(xin, toep_ref, box_ref, filt, mag):
    n = CROWS
    zero = jnp.zeros((n, 256), BF16)
    parts = [xin[q, :, 256 * k : 256 * k + 256] for q in range(4) for k in range(4)]
    x0 = jnp.concatenate([zero] + parts, axis=0)
    x1 = jnp.concatenate(parts + [zero], axis=0)
    filtered = (mm(x0, toep_ref[0, 0]) + mm(x1, toep_ref[1, 0])) + (
        mm(x0, toep_ref[0, 1]) + mm(x1, toep_ref[1, 1])
    )
    filt[...] = filtered.reshape(17, n, 256)
    high, low = split(jnp.abs(filtered))
    mag[0] = high.reshape(17, n, 256)
    mag[1] = low.reshape(17, n, 256)
    level = (
        mm(mag[0, 0:16].reshape(16 * n, 256), box_ref[0])
        + mm(mag[0, 1:17].reshape(16 * n, 256), box_ref[1])
    ) + (
        mm(mag[1, 0:16].reshape(16 * n, 256), box_ref[0])
        + mm(mag[1, 1:17].reshape(16 * n, 256), box_ref[1])
    )
    center = jnp.concatenate([filt[0:16, :, 128:256], filt[1:17, :, 0:128]], axis=-1)
    return center / (level.reshape(16, n, 256) * (1.0 / (2 * NH + 1)) + 1e-05)


def combine_quarters(normed):
    n = CROWS
    seg = normed.reshape(4, 4, n, 256)
    even, odd = seg[0] + seg[2], seg[1] + seg[3]
    flat = lambda v: jnp.concatenate([v[k] for k in range(4)], axis=-1)
    rows = [flat(even + odd), flat(even - odd)]
    rows += [jnp.concatenate([flat(seg[0] - seg[2]), flat(seg[1] - seg[3])], axis=0)]
    return [jnp.concatenate(split(value), axis=0) for value in rows]


def spectra_of(parts, tab_ref, half):
    n = CROWS
    cols = slice(256 * half, 256 * half + 256)

    def transform(both, r):
        rows = both.shape[0] // 2
        full = mm(both, tab_ref[0, r, :, cols])
        return full[:rows] + full[rows:] + mm(both[:rows], tab_ref[1, r, :, cols])

    s0, s2 = transform(parts[0], 0), transform(parts[1], 1)
    odd1, odd3 = transform(parts[2], 2), transform(parts[2], 3)
    lane = lax.broadcasted_iota(jnp.int32, (n, 256), 1)
    sign = jnp.where((lane // 64) % 2 == 0, 1.0, -1.0)

    def swap(value):
        return jnp.concatenate(
            [pltpu.roll(value[:, 128 * s : 128 * s + 128], 64, 1) for s in range(2)], axis=-1
        )

    s1 = odd1[:n] + sign * swap(odd1[n:])
    s3 = odd3[:n] - sign * swap(odd3[n:])
    return s0, s1, s2, s3


def whiten(spectra, stage, out_ref, half):
    n = CROWS
    power = sum(s * s for s in spectra)
    li = lax.broadcasted_iota(jnp.int32, (128, 128), 0)
    lj = lax.broadcasted_iota(jnp.int32, (128, 128), 1)
    group = jnp.where((li // 16) % 4 == (lj // 16) % 4, 1.0, 0.0).astype(BF16)
    tall = jnp.concatenate([power[:, 128 * s : 128 * s + 128] for s in range(2)], axis=0)
    high, low = split(tall)
    band = mm(high, group) + mm(low, group)
    scale = lax.rsqrt(band * (1.0 / WB) + 1e-06)
    slot = (lax.broadcasted_iota(jnp.int32, (n, 128), 1) // 16) % 4
    for s in range(2):
        sc = scale[n * s : n * s + n]
        parts = [spectra[r][:, 128 * s : 128 * s + 128] * sc for r in range(4)]
        for b in range(4):
            value = None
            for r in range(4):
                moved = parts[r] if r == b else pltpu.roll(parts[r], (16 * (r - b)) % 128, 1)
                value = moved if value is None else jnp.where(slot == r, moved, value)
            for k in range(4):
                stage[s, BLK * k + BR * b : BLK * k + BR * b + BR, :] = value[BR * k : BR * k + BR]
        out_ref[2 * half + s] = stage[s].astype(BF16).reshape(4, BLK, 128)


def column_masks(count_ref, mask_ref, valid_ref):
    row = (lax.broadcasted_iota(jnp.int32, (144, 128), 0) * 10923) >> 17
    lane = lax.broadcasted_iota(jnp.int32, (144, 128), 1)
    for cg in range(3):
        column = ((lane + 128 * cg) * 10923) >> 17
        mask_ref[cg] = jnp.where(row + 2 * (128 * cg // 24) == column, 1.0, 0.0)
    tile = lax.broadcasted_iota(jnp.int32, (128, 1536), 0)
    column = lax.broadcasted_iota(jnp.int32, (128, 1536), 1)
    offset = column - BR * tile
    spread = jnp.where((offset >= 0) & (offset < BR), 1.0, 0.0).astype(BF16)
    counts = jnp.broadcast_to(count_ref[...].astype(F32), (8, 128)).astype(BF16)
    column = lax.broadcasted_iota(jnp.int32, (8, 1536), 1)
    station = ((column - BR * ((column * 10923) >> 17)) * 10923) >> 15
    valid_ref[...] = jnp.where(station.astype(F32) < mm(counts, spread), 1.0 / WB, 0.0)


def gather_ends(got, ends, z, w, left, right, turned):
    sign = jnp.where(lax.broadcasted_iota(jnp.int32, (BLK, 128), 1) < 64, -1.0, 1.0)

    def place(end):
        step = ((end >> 8) - z) & (NZ - 1)
        order = jnp.where(step < NZ // 2, 2 * step, 2 * NZ - 1 - 2 * step)
        return ((end >> 5) & (PLANE - 1)) * NZ + order

    def four(g, carry):
        rows = pl.ds(pl.multiple_of(BLK * g, 16), BLK)
        for e in range(2):
            tiles = [got[place(ends[2 * w + e, 4 * g + k])].astype(F32) for k in range(4)]
            for b in range(4):
                value = jnp.concatenate([t[BR * b : BR * b + BR] for t in tiles], axis=0)
                if e == 0:
                    left[b, rows] = value.astype(BF16)
                else:
                    right[b, rows] = value.astype(BF16)
                    turned[b, rows] = (sign * pltpu.roll(value, 64, 1)).astype(BF16)
        return carry

    lax.fori_loop(0, 32, four, 0, unroll=8)


def tile_products(left, right, turned, mask_ref, valid_ref, out_ref):
    for b in range(4):
        for cg in range(12):
            first = 2 * (128 * cg // 24)
            rows = left[b, BR * first : BR * first + 144]
            cols = slice(128 * cg, 128 * cg + 128)
            other = jnp.concatenate([right[b, cols], turned[b, cols]], axis=0)
            full = lax.dot_general(
                rows, other, (((1,), (1,)), ((), ())), preferred_element_type=F32
            )
            total = jnp.zeros((24, 256), F32)
            for k in range(6):
                keep = mask_ref[cg % 3, 24 * k : 24 * k + 24]
                total += jnp.concatenate([keep, keep], axis=1) * full[24 * k : 24 * k + 24]
            short = total[:BR] + total[BR:]
            valid = valid_ref[0:1, cols]
            out_ref[b, :, 0, cols] = short[:, :128] * valid
            out_ref[b, :, 1, cols] = short[:, 128:] * valid


def whole_kernel(
    raw_ref, taps_hbm, ends_hbm, count_hbm, tab_hbm, out_ref,
    taps_ref, ends_ref, count_ref, wide, tab, xin, toep, box, filt, mag, stage, wsend, pick_v, pick_s, ends_s,
    near_stage, far_stage, got, left, right, turned, mask, valid,
    slot0, slot1, slot2, slot3, slot4, slot5, slot6, slot7, slot8,
    tab_sem, own_sem, xs_sem, xr_sem, bs_sem, br_sem, zs_sem, zr_sem,
    ps_sem, pr_sem, pk_sem,
):
    slots = (slot0, slot1, slot2, slot3, slot4, slot5, slot6, slot7, slot8)
    sta = lax.axis_index("sta")
    x = lax.axis_index("sec")
    z = sta // PLANE
    w = sta % PLANE

    def at(step, ww):
        return ((z + step + NZ) % NZ) * PLANE + ww

    def xpeer(i):
        return (x + i) % NX

    def from_x(i):
        return (x + NX - i) % NX

    barrier = pltpu.get_barrier_semaphore()

    def greet(peer):
        pl.semaphore_signal(barrier, inc=1, device_id=peer, device_id_type=MESH)

    for i in range(1, NX):
        greet((sta, xpeer(i)))
    greet((at(1, w), x))
    greet((at(-1, w), x))
    for i in range(1, PLANE):
        greet((at(0, (w + i) % PLANE), x))

    taps_copy = pltpu.make_async_copy(taps_hbm, taps_ref, pk_sem.at[2])
    taps_copy.start()
    all_ends_copy = pltpu.make_async_copy(ends_hbm, ends_ref, pk_sem.at[3])
    all_ends_copy.start()
    count_copy = pltpu.make_async_copy(count_hbm, count_ref, pk_sem.at[4])
    count_copy.start()
    tab_copy = pltpu.make_async_copy(tab_hbm, wide, tab_sem)
    ends_copy = pltpu.make_async_copy(
        ends_hbm.at[pl.ds(pl.multiple_of(16 * z, 16), 16)], ends_s, pk_sem.at[0]
    )
    ends_copy.start()

    def raw_rows(q, c):
        return raw_ref.at[pl.ds(pl.multiple_of(96 * q + CROWS * c, 16), CROWS)]

    def own_copy(c):
        return pltpu.make_async_copy(raw_rows(x, c), xin.at[c, x], own_sem.at[c])

    for c in range(2):
        own_copy(c).start()
    pl.semaphore_wait(barrier, NX - 1 + 2 + PLANE - 1)

    def raw_copy(c, i):
        return pltpu.make_async_remote_copy(
            src_ref=raw_rows(xpeer(i), c),
            dst_ref=xin.at[c, x],
            send_sem=xs_sem.at[c, i - 1],
            recv_sem=xr_sem.at[c, i - 1],
            device_id=(sta, xpeer(i)),
            device_id_type=MESH,
        )

    def raw_start(c):
        for i in (2, 1, 3):
            raw_copy(c, i).start()

    def raw_wait(c):
        own_copy(c).wait()
        for i in range(1, NX):
            dst = xin.at[c, from_x(i)]
            pltpu.make_async_copy(dst, dst, xr_sem.at[c, i - 1]).wait()

    raw_start(0)
    raw_start(1)
    tab_copy.start()

    taps_copy.wait()
    build_filters(taps_ref, toep, box)
    all_ends_copy.wait()
    lane = lax.broadcasted_iota(jnp.int32, (16, 128), 1)
    picks = jnp.zeros((16, 128), jnp.int32)

    def asked(step, source):
        rows = ends_ref[pl.ds(pl.multiple_of(16 * ((z + step + NZ) % NZ), 16), 16), :]
        return jnp.max(jnp.where(rows // 32 == source, rows % 32, 0), axis=1, keepdims=True)

    wanted = [(0, at(-s if s <= REACH else s - REACH, w)) for s in range(9)]
    wanted += [(h, at(-REACH, w)) for h in range(1, REACH + 1)]
    wanted += [(-h, at(REACH, w)) for h in range(1, REACH + 1)]
    for col, (step, source) in enumerate(wanted):
        picks = jnp.where(lane == col, asked(step, source), picks)
    pick_v[...] = picks
    pick_copy = pltpu.make_async_copy(pick_v, pick_s, pk_sem.at[1])
    pick_copy.start()
    count_copy.wait()
    column_masks(count_ref, mask, valid)
    tab_copy.wait()
    split_tables(wide, tab)
    pick_copy.wait()
    ends_copy.wait()

    def back_copy(c, s):
        i = (s - x + NX) % NX
        return pltpu.make_async_remote_copy(
            src_ref=wsend.at[c, s],
            dst_ref=slot0.at[pl.ds(8 * x + 4 * c, 4)],
            send_sem=bs_sem.at[c, i],
            recv_sem=br_sem.at[c, i],
            device_id=(sta, s),
            device_id_type=MESH,
        )

    def section_start(c, half):
        for s in (2 * half, 2 * half + 1):

            @pl.when(s != x)
            def _():
                back_copy(c, s).start()

    def back_wait(c, i):
        rows = slot0.at[pl.ds(8 * from_x(i) + 4 * c, 4)]
        pltpu.make_async_copy(rows, rows, br_sem.at[c, i]).wait()

    def ring_wait(d, h, c, i):
        rows = slots[h + 4 * d].at[pl.ds(8 * from_x(i) + 4 * c, 4)]
        pltpu.make_async_copy(rows, rows, zr_sem.at[d, h - 1, 4 * c + i]).wait()

    def ring_copy(d, h, c, i):
        rows = pl.ds(8 * from_x(i) + 4 * c, 4)
        return pltpu.make_async_remote_copy(
            src_ref=(slots[0] if h == 1 else slots[h - 1 + 4 * d]).at[rows],
            dst_ref=slots[h + 4 * d].at[rows],
            send_sem=zs_sem.at[d, h - 1, 4 * c + i],
            recv_sem=zr_sem.at[d, h - 1, 4 * c + i],
            device_id=(at(1 - 2 * d, w), x),
            device_id_type=MESH,
        )

    def ring_start(h, c, i):
        for d in range(2):
            if h > 1:
                ring_wait(d, h - 1, c, i)
            ring_copy(d, h, c, i).start()

    def first_start(c):
        for i in range(1, NX):
            back_wait(c, i)
            ring_start(1, c, i)

    def asked_block(ww, col):
        return jnp.clip(jnp.maximum(pick_s[2 * ww, col], pick_s[2 * ww + 1, col]), 0, 31)

    def place_copy(source, place, step, ww):
        return pltpu.make_async_remote_copy(
            src_ref=source,
            dst_ref=got.at[w * NZ + place],
            send_sem=ps_sem,
            recv_sem=pr_sem,
            device_id=(at(step, ww), x),
            device_id_type=MESH,
        )

    def near_picks(s):
        place = 0 if s == 0 else (2 * s - 1 if s <= REACH else 2 * (s - REACH))

        def one(i, carry):
            ww = (w + i) % PLANE
            near_stage[s, i] = slots[s][asked_block(ww, s)]
            place_copy(near_stage.at[s, i], place, 0, ww).start()
            return carry

        lax.fori_loop(1, PLANE, one, 0)
        got[w * NZ + place] = slots[s][asked_block(w, s)]

    def far_picks(d, k):
        col = 9 + 4 * d + k - 1
        place = 2 * (REACH + k) - 1 + (d if k < REACH else 0)
        block = slots[REACH + 4 * d]

        def one(i, carry):
            ww = i if k < REACH else 2 * i + d
            far_stage[d, k - 1, i] = block[asked_block(ww, col)]
            place_copy(far_stage.at[d, k - 1, i], place, k * (1 - 2 * d), ww).start()
            return carry

        lax.fori_loop(0, PLANE if k < REACH else PLANE // 2, one, 0)

    for c in range(2):
        raw_wait(c)
        parts = combine_quarters(normalize(xin.at[c], toep, box, filt, mag))
        whiten(spectra_of(parts, tab, 0), stage, wsend.at[c], 0)
        section_start(c, 0)
        if c == 1:
            first_start(0)
        whiten(spectra_of(parts, tab, 1), stage, wsend.at[c], 1)
        section_start(c, 1)
        slot0[pl.ds(8 * x + 4 * c, 4)] = wsend[c, x]
        ring_start(1, c, 0)
    for i in range(NX):
        ring_start(2, 0, i)
    first_start(1)
    for i in range(NX):
        ring_start(2, 1, i)
    near_picks(0)
    near_picks(1)
    near_picks(1 + REACH)
    for h in range(3, REACH + 1):
        for c in range(2):
            for i in range(NX):
                ring_start(h, c, i)
        near_picks(h - 1)
        near_picks(h - 1 + REACH)
    for c in range(2):
        for i in range(NX):
            for d in range(2):
                ring_wait(d, REACH, c, i)
    for k in range(REACH, 0, -1):
        for d in range(2):
            far_picks(d, k)
    near_picks(REACH)
    near_picks(2 * REACH)

    pltpu.make_async_copy(got.at[0:119], got.at[0:119], pr_sem).wait()
    gather_ends(got, ends_s, z, w, left, right, turned)
    tile_products(left, right, turned, mask, valid, out_ref)

    pltpu.make_async_copy(got.at[0:119], got.at[0:119], ps_sem).wait()
    for c in range(2):
        for i in range(1, NX):
            raw_copy(c, i).wait_send()
            back_copy(c, xpeer(i)).wait_send()
        for i in range(NX):
            for d in range(2):
                for h in range(1, REACH + 1):
                    ring_copy(d, h, c, i).wait_send()


def body(raw, taps, pairs, counts):
    ends = pairs.reshape(128, 128, 2).transpose(0, 2, 1).reshape(256, 128)
    any_spec = pl.BlockSpec(memory_space=pl.ANY)
    vmem = pl.BlockSpec(memory_space=pltpu.VMEM)
    dma = pltpu.SemaphoreType.DMA
    tiles = pltpu.VMEM((4, 1536, 128), BF16)
    result = pl.pallas_call(
        whole_kernel,
        out_shape=jax.ShapeDtypeStruct((4, BR, 2, 1536), F32),
        in_specs=[any_spec] * 5,
        out_specs=vmem,
        scratch_shapes=[
            pltpu.SMEM((33,), F32),
            pltpu.VMEM((256, 128), jnp.int32),
            pltpu.VMEM((1, 128), jnp.int32),
            pltpu.VMEM((4096, 512), F32),
            pltpu.VMEM((2, 4, 1024, 512), BF16),
            pltpu.VMEM((2, NX, CROWS, 1024), BF16),
            pltpu.VMEM((2, 2, 256, 256), BF16),
            pltpu.VMEM((2, 256, 256), BF16),
            pltpu.VMEM((17, CROWS, 256), F32),
            pltpu.VMEM((2, 17, CROWS, 256), BF16),
            pltpu.VMEM((4, 4 * BLK, 128), F32),
            pltpu.VMEM((2, 4, 4, BLK, 128), BF16),
            pltpu.VMEM((16, 128), jnp.int32),
            pltpu.SMEM((16, 128), jnp.int32),
            pltpu.SMEM((16, 128), jnp.int32),
            pltpu.VMEM((9, PLANE, BLK, 128), BF16),
            pltpu.VMEM((2, REACH, PLANE, BLK, 128), BF16),
            pltpu.VMEM((NZ * PLANE, BLK, 128), BF16),
            tiles, tiles, tiles,
            pltpu.VMEM((3, 144, 128), F32),
            pltpu.VMEM((8, 1536), F32),
        ]
        + [pltpu.VMEM((32, BLK, 128), BF16)] * 9
        + [
            dma, dma((2,)), dma((2, 3)), dma((2, 3)), dma((2, 4)), dma((2, 4)),
            dma((2, 4, 8)), dma((2, 4, 8)), dma, dma, dma((5,)),
        ],
        compiler_params=pltpu.CompilerParams(
            collective_id=0, has_side_effects=True, vmem_limit_bytes=60 << 20
        ),
        name="cross_spectra",
    )(raw, taps, ends, counts.reshape(1, 128), jnp.asarray(dft_tables()))
    return result.transpose(0, 2, 1, 3)


def solution(mesh):
    return jax.shard_map(
        body,
        mesh=mesh,
        in_specs=(P("sta", "sec"), P(), P(), P("sta")),
        out_specs=P("sec", None, None, "sta"),
        check_vma=False,
    )
```

```python
import functools
import math

import jax
import jax.numpy as jnp
import numpy as np
from jax import lax
from jax.experimental import pallas as pl
from jax.experimental.pallas import tpu as pltpu
from jax.sharding import PartitionSpec as P

MESH = pl.DeviceIdType.MESH
L = 4096
F = 1024
LOWBIN = 4
WB = 64
FH = 16
NH = 32
BR = 12
PLANE = 8
NZ = 16
NX = 4
REACH = 4
CROWS = 48
BLK = 4 * BR
F32 = jnp.float32
BF16 = jnp.bfloat16


def dft_tables():
    cols = np.arange(512)
    sect, part, band, mm = cols // 128, (cols // 64) % 2, (cols // 16) % 4, cols % 16
    m = (4 * sect + band) * 16 + mm + 1
    t = np.arange(1024)
    planes = []
    for r in (0, 2, 1, 3):
        angle = 2.0 * np.pi / L * ((t[:, None] * (4 * m + r)[None, :]) % L)
        planes.append(np.where(part[None, :] == 0, np.cos(angle), -np.sin(angle)))
    return np.concatenate(planes).astype(np.float32)


def split(value):
    high = value.astype(BF16)
    return high, (value - high.astype(F32)).astype(BF16)


def mm(a, b):
    return jnp.dot(a, b, preferred_element_type=F32)


def build_filters(taps_ref, toep_ref, box_ref):
    def rows(i, carry):
        start = pl.multiple_of(32 * i, 32)
        diff = (
            lax.broadcasted_iota(jnp.int32, (32, 256), 0)
            + 32 * i
            - lax.broadcasted_iota(jnp.int32, (32, 256), 1)
        )
        first = jnp.zeros((32, 256), F32)
        second = jnp.zeros((32, 256), F32)
        for k in range(2 * FH + 1):
            tap = taps_ref[k]
            first = jnp.where(diff == k + 112, tap, first)
            second = jnp.where(diff == k - 144, tap, second)
        for which, value in enumerate((first, second)):
            high, low = split(value)
            toep_ref[which, 0, pl.ds(start, 32)] = high
            toep_ref[which, 1, pl.ds(start, 32)] = low
        box_ref[0, pl.ds(start, 32)] = jnp.where(jnp.abs(diff - 128) <= NH, 1.0, 0.0).astype(BF16)
        box_ref[1, pl.ds(start, 32)] = jnp.where(jnp.abs(diff + 128) <= NH, 1.0, 0.0).astype(BF16)
        return carry

    lax.fori_loop(0, 8, rows, 0)


def split_tables(wide, tab_ref):
    def rows(i, carry):
        start = pl.multiple_of(32 * i, 32)
        for r in range(4):
            high, low = split(wide[pl.ds(1024 * r + start, 32)])
            tab_ref[0, r, pl.ds(start, 32)] = high
            tab_ref[1, r, pl.ds(start, 32)] = low
        return carry

    lax.fori_loop(0, 32, rows, 0)


def normalize(xin, toep_ref, box_ref, filt, mag):
    n = CROWS
    zero = jnp.zeros((n, 256), BF16)
    parts = [xin[q, :, 256 * k : 256 * k + 256] for q in range(4) for k in range(4)]
    x0 = jnp.concatenate([zero] + parts, axis=0)
    x1 = jnp.concatenate(parts + [zero], axis=0)
    filtered = (mm(x0, toep_ref[0, 0]) + mm(x1, toep_ref[1, 0])) + (
        mm(x0, toep_ref[0, 1]) + mm(x1, toep_ref[1, 1])
    )
    filt[...] = filtered.reshape(17, n, 256)
    high, low = split(jnp.abs(filtered))
    mag[0] = high.reshape(17, n, 256)
    mag[1] = low.reshape(17, n, 256)
    level = (
        mm(mag[0, 0:16].reshape(16 * n, 256), box_ref[0])
        + mm(mag[0, 1:17].reshape(16 * n, 256), box_ref[1])
    ) + (
        mm(mag[1, 0:16].reshape(16 * n, 256), box_ref[0])
        + mm(mag[1, 1:17].reshape(16 * n, 256), box_ref[1])
    )
    center = jnp.concatenate([filt[0:16, :, 128:256], filt[1:17, :, 0:128]], axis=-1)
    return center / (level.reshape(16, n, 256) * (1.0 / (2 * NH + 1)) + 1e-05)


def combine_quarters(normed):
    n = CROWS
    seg = normed.reshape(4, 4, n, 256)
    even, odd = seg[0] + seg[2], seg[1] + seg[3]
    flat = lambda v: jnp.concatenate([v[k] for k in range(4)], axis=-1)
    rows = [flat(even + odd), flat(even - odd)]
    rows += [jnp.concatenate([flat(seg[0] - seg[2]), flat(seg[1] - seg[3])], axis=0)]
    return [jnp.concatenate(split(value), axis=0) for value in rows]


def spectra_of(parts, tab_ref, half):
    n = CROWS
    cols = pl.ds(pl.multiple_of(256 * half, 256), 256)

    def transform(both, r):
        rows = both.shape[0] // 2
        full = mm(both, tab_ref[0, r, :, cols])
        return full[:rows] + full[rows:] + mm(both[:rows], tab_ref[1, r, :, cols])

    s0, s2 = transform(parts[0], 0), transform(parts[1], 1)
    odd1, odd3 = transform(parts[2], 2), transform(parts[2], 3)
    lane = lax.broadcasted_iota(jnp.int32, (n, 256), 1)
    sign = jnp.where((lane // 64) % 2 == 0, 1.0, -1.0)

    def swap(value):
        return jnp.concatenate(
            [pltpu.roll(value[:, 128 * s : 128 * s + 128], 64, 1) for s in range(2)], axis=-1
        )

    s1 = odd1[:n] + sign * swap(odd1[n:])
    s3 = odd3[:n] - sign * swap(odd3[n:])
    return s0, s1, s2, s3


def whiten(spectra, stage, out_ref, half):
    n = CROWS
    power = sum(s * s for s in spectra)
    li = lax.broadcasted_iota(jnp.int32, (128, 128), 0)
    lj = lax.broadcasted_iota(jnp.int32, (128, 128), 1)
    group = jnp.where((li // 16) % 4 == (lj // 16) % 4, 1.0, 0.0).astype(BF16)
    tall = jnp.concatenate([power[:, 128 * s : 128 * s + 128] for s in range(2)], axis=0)
    high, low = split(tall)
    band = mm(high, group) + mm(low, group)
    scale = lax.rsqrt(band * (1.0 / WB) + 1e-06)
    slot = (lax.broadcasted_iota(jnp.int32, (n, 128), 1) // 16) % 4
    for s in range(2):
        sc = scale[n * s : n * s + n]
        parts = [spectra[r][:, 128 * s : 128 * s + 128] * sc for r in range(4)]
        for b in range(4):
            value = None
            for r in range(4):
                moved = parts[r] if r == b else pltpu.roll(parts[r], (16 * (r - b)) % 128, 1)
                value = moved if value is None else jnp.where(slot == r, moved, value)
            for k in range(4):
                stage[s, BLK * k + BR * b : BLK * k + BR * b + BR, :] = value[BR * k : BR * k + BR]
        out_ref[2 * half + s] = stage[s].astype(BF16).reshape(4, BLK, 128)


def column_masks(count_ref, mask_ref, valid_ref):
    row = (lax.broadcasted_iota(jnp.int32, (144, 128), 0) * 10923) >> 17
    lane = lax.broadcasted_iota(jnp.int32, (144, 128), 1)
    for cg in range(3):
        column = ((lane + 128 * cg) * 10923) >> 17
        mask_ref[cg] = jnp.where(row + 2 * (128 * cg // 24) == column, 1.0, 0.0)
    tile = lax.broadcasted_iota(jnp.int32, (128, 1536), 0)
    column = lax.broadcasted_iota(jnp.int32, (128, 1536), 1)
    offset = column - BR * tile
    spread = jnp.where((offset >= 0) & (offset < BR), 1.0, 0.0).astype(BF16)
    counts = jnp.broadcast_to(count_ref[...].astype(F32), (8, 128)).astype(BF16)
    column = lax.broadcasted_iota(jnp.int32, (8, 1536), 1)
    station = ((column - BR * ((column * 10923) >> 17)) * 10923) >> 15
    valid_ref[...] = jnp.where(station.astype(F32) < mm(counts, spread), 1.0 / WB, 0.0)


def gather_ends(got, ends, z, w, left, right, turned):
    sign = jnp.where(lax.broadcasted_iota(jnp.int32, (BLK, 128), 1) < 64, -1.0, 1.0)

    def place(end):
        step = ((end >> 8) - z) & (NZ - 1)
        order = jnp.where(step < NZ // 2, 2 * step, 2 * NZ - 1 - 2 * step)
        return ((end >> 5) & (PLANE - 1)) * NZ + order

    def four(g, carry):
        rows = pl.ds(pl.multiple_of(BLK * g, 16), BLK)
        for e in range(2):
            tiles = [got[place(ends[2 * w + e, 4 * g + k])].astype(F32) for k in range(4)]
            for b in range(4):
                value = jnp.concatenate([t[BR * b : BR * b + BR] for t in tiles], axis=0)
                if e == 0:
                    left[b, rows] = value.astype(BF16)
                else:
                    right[b, rows] = value.astype(BF16)
                    turned[b, rows] = (sign * pltpu.roll(value, 64, 1)).astype(BF16)
        return carry

    lax.fori_loop(0, 32, four, 0, unroll=8)


def tile_products(left, right, turned, mask_ref, valid_ref, made, out_ref, out_sem):
    for b in range(4):
        for cg in range(12):
            first = 2 * (128 * cg // 24)
            rows = left[b, BR * first : BR * first + 144]
            cols = slice(128 * cg, 128 * cg + 128)
            other = jnp.concatenate([right[b, cols], turned[b, cols]], axis=0)
            full = lax.dot_general(
                rows, other, (((1,), (1,)), ((), ())), preferred_element_type=F32
            )
            total = jnp.zeros((24, 256), F32)
            for k in range(6):
                keep = mask_ref[cg % 3, 24 * k : 24 * k + 24]
                total += jnp.concatenate([keep, keep], axis=1) * full[24 * k : 24 * k + 24]
            short = total[:BR] + total[BR:]
            valid = valid_ref[0:1, cols]
            made[b, :, 0, cols] = short[:, :128] * valid
            made[b, :, 1, cols] = short[:, 128:] * valid
        pltpu.make_async_copy(made.at[b], out_ref.at[b], out_sem.at[b]).start()


def whole_kernel(
    raw_ref, taps_hbm, ends_hbm, count_hbm, tab_hbm, out_ref,
    taps_ref, ends_ref, count_ref, wide, tab, xin, toep, box, filt, mag, stage, wsend, pick_v, pick_s, ends_s,
    near_stage, far_stage, got, left, right, turned, mask, valid, made,
    slot0, slot1, slot2, slot3, slot4, slot5, slot6, slot7, slot8,
    tab_sem, own_sem, xs_sem, xr_sem, bs_sem, br_sem, zs_sem, zr_sem,
    ps_sem, pr_sem, pk_sem, out_sem,
):
    slots = (slot0, slot1, slot2, slot3, slot4, slot5, slot6, slot7, slot8)
    sta = lax.axis_index("sta")
    x = lax.axis_index("sec")
    z = sta // PLANE
    w = sta % PLANE

    def at(step, ww):
        return ((z + step + NZ) % NZ) * PLANE + ww

    def xpeer(i):
        return (x + i) % NX

    def from_x(i):
        return (x + NX - i) % NX

    barrier = pltpu.get_barrier_semaphore()

    def greet(peer):
        pl.semaphore_signal(barrier, inc=1, device_id=peer, device_id_type=MESH)

    for i in range(1, NX):
        greet((sta, xpeer(i)))
    greet((at(1, w), x))
    greet((at(-1, w), x))
    for i in range(1, PLANE):
        greet((at(0, (w + i) % PLANE), x))

    taps_copy = pltpu.make_async_copy(taps_hbm, taps_ref, pk_sem.at[2])
    taps_copy.start()
    all_ends_copy = pltpu.make_async_copy(ends_hbm, ends_ref, pk_sem.at[3])
    all_ends_copy.start()
    count_copy = pltpu.make_async_copy(count_hbm, count_ref, pk_sem.at[4])
    count_copy.start()
    tab_copy = pltpu.make_async_copy(tab_hbm, wide, tab_sem)
    ends_copy = pltpu.make_async_copy(
        ends_hbm.at[pl.ds(pl.multiple_of(16 * z, 16), 16)], ends_s, pk_sem.at[0]
    )
    ends_copy.start()

    def raw_rows(q, c):
        return raw_ref.at[pl.ds(pl.multiple_of(96 * q + CROWS * c, 16), CROWS)]

    def own_copy(c):
        return pltpu.make_async_copy(raw_rows(x, c), xin.at[c, x], own_sem.at[c])

    for c in range(2):
        own_copy(c).start()
    pl.semaphore_wait(barrier, NX - 1 + 2 + PLANE - 1)

    def raw_copy(c, i):
        return pltpu.make_async_remote_copy(
            src_ref=raw_rows(xpeer(i), c),
            dst_ref=xin.at[c, x],
            send_sem=xs_sem.at[c, i - 1],
            recv_sem=xr_sem.at[c, i - 1],
            device_id=(sta, xpeer(i)),
            device_id_type=MESH,
        )

    def raw_start(c):
        for i in (2, 1, 3):
            raw_copy(c, i).start()

    def raw_wait(c):
        own_copy(c).wait()
        for i in range(1, NX):
            dst = xin.at[c, from_x(i)]
            pltpu.make_async_copy(dst, dst, xr_sem.at[c, i - 1]).wait()

    raw_start(0)
    tab_copy.start()

    taps_copy.wait()
    build_filters(taps_ref, toep, box)
    all_ends_copy.wait()
    lane = lax.broadcasted_iota(jnp.int32, (16, 128), 1)
    picks = jnp.zeros((16, 128), jnp.int32)

    def asked(step, source):
        rows = ends_ref[pl.ds(pl.multiple_of(16 * ((z + step + NZ) % NZ), 16), 16), :]
        return jnp.max(jnp.where(rows // 32 == source, rows % 32, 0), axis=1, keepdims=True)

    wanted = [(0, at(-s if s <= REACH else s - REACH, w)) for s in range(9)]
    wanted += [(h, at(-REACH, w)) for h in range(1, REACH + 1)]
    wanted += [(-h, at(REACH, w)) for h in range(1, REACH + 1)]
    for col, (step, source) in enumerate(wanted):
        picks = jnp.where(lane == col, asked(step, source), picks)
    pick_v[...] = picks
    pick_copy = pltpu.make_async_copy(pick_v, pick_s, pk_sem.at[1])
    pick_copy.start()
    count_copy.wait()
    column_masks(count_ref, mask, valid)
    raw_start(1)
    tab_copy.wait()
    split_tables(wide, tab)
    pick_copy.wait()
    ends_copy.wait()

    def back_copy(c, s):
        i = (s - x + NX) % NX
        return pltpu.make_async_remote_copy(
            src_ref=wsend.at[c, s],
            dst_ref=slot0.at[pl.ds(8 * x + 4 * c, 4)],
            send_sem=bs_sem.at[c, i],
            recv_sem=br_sem.at[c, i],
            device_id=(sta, s),
            device_id_type=MESH,
        )

    def first_copy(d, s):
        i = (s - x + NX) % NX
        return pltpu.make_async_remote_copy(
            src_ref=wsend.at[0, s],
            dst_ref=slots[1 + 4 * d].at[pl.ds(8 * x, 4)],
            send_sem=zs_sem.at[d, 0, i],
            recv_sem=zr_sem.at[d, 0, i],
            device_id=(at(1 - 2 * d, w), s),
            device_id_type=MESH,
        )

    def section_start(c, half):
        if c == 0:
            for s in (2 * half, 2 * half + 1):
                for d in range(2):
                    first_copy(d, s).start()
        for s in (2 * half, 2 * half + 1):

            @pl.when(s != x)
            def _():
                back_copy(c, s).start()

    def back_wait(c, i):
        rows = slot0.at[pl.ds(8 * from_x(i) + 4 * c, 4)]
        pltpu.make_async_copy(rows, rows, br_sem.at[c, i]).wait()

    def ring_wait(d, h, c, i):
        rows = slots[h + 4 * d].at[pl.ds(8 * from_x(i) + 4 * c, 4)]
        pltpu.make_async_copy(rows, rows, zr_sem.at[d, h - 1, 4 * c + i]).wait()

    def ring_copy(d, h, c, i):
        rows = pl.ds(8 * from_x(i) + 4 * c, 4)
        return pltpu.make_async_remote_copy(
            src_ref=(slots[0] if h == 1 else slots[h - 1 + 4 * d]).at[rows],
            dst_ref=slots[h + 4 * d].at[rows],
            send_sem=zs_sem.at[d, h - 1, 4 * c + i],
            recv_sem=zr_sem.at[d, h - 1, 4 * c + i],
            device_id=(at(1 - 2 * d, w), x),
            device_id_type=MESH,
        )

    def ring_start(h, c, i):
        for d in range(2):
            if h > 1:
                ring_wait(d, h - 1, c, i)
            ring_copy(d, h, c, i).start()

    def first_start(c):
        for i in range(1, NX):
            back_wait(c, i)
            ring_start(1, c, i)

    def asked_block(ww, col):
        return jnp.clip(jnp.maximum(pick_s[2 * ww, col], pick_s[2 * ww + 1, col]), 0, 31)

    def place_copy(source, place, step, ww):
        return pltpu.make_async_remote_copy(
            src_ref=source,
            dst_ref=got.at[w * NZ + place],
            send_sem=ps_sem,
            recv_sem=pr_sem,
            device_id=(at(step, ww), x),
            device_id_type=MESH,
        )

    def near_picks(s):
        place = 0 if s == 0 else (2 * s - 1 if s <= REACH else 2 * (s - REACH))

        def one(i, carry):
            ww = (w + i) % PLANE
            near_stage[s, i] = slots[s][asked_block(ww, s)]
            place_copy(near_stage.at[s, i], place, 0, ww).start()
            return carry

        lax.fori_loop(1, PLANE, one, 0)
        got[w * NZ + place] = slots[s][asked_block(w, s)]

    def far_picks(d, k):
        col = 9 + 4 * d + k - 1
        place = 2 * (REACH + k) - 1 + (d if k < REACH else 0)
        block = slots[REACH + 4 * d]

        def one(i, carry):
            ww = i if k < REACH else 2 * i + d
            far_stage[d, k - 1, i] = block[asked_block(ww, col)]
            place_copy(far_stage.at[d, k - 1, i], place, k * (1 - 2 * d), ww).start()
            return carry

        lax.fori_loop(0, PLANE if k < REACH else PLANE // 2, one, 0)

    mine = x // 2
    for c in range(2):
        raw_wait(c)
        parts = combine_quarters(normalize(xin.at[c], toep, box, filt, mag))
        whiten(spectra_of(parts, tab, mine), stage, wsend.at[c], mine)
        section_start(c, mine)
        slot0[pl.ds(8 * x + 4 * c, 4)] = wsend[c, x]
        if c == 1:
            ring_start(1, 1, 0)
            for i in range(NX):
                ring_start(2, 0, i)
        whiten(spectra_of(parts, tab, 1 - mine), stage, wsend.at[c], 1 - mine)
        section_start(c, 1 - mine)
    for i in range(1, NX):
        back_wait(0, i)
    first_start(1)
    for i in range(NX):
        ring_start(2, 1, i)
    near_picks(0)
    near_picks(1)
    near_picks(1 + REACH)
    for h in range(3, REACH + 1):
        for c in range(2):
            for i in range(NX):
                ring_start(h, c, i)
        near_picks(h - 1)
        near_picks(h - 1 + REACH)
    for c in range(2):
        for i in range(NX):
            for d in range(2):
                ring_wait(d, REACH, c, i)
    for k in range(REACH, 0, -1):
        for d in range(2):
            far_picks(d, k)
    near_picks(REACH)
    near_picks(2 * REACH)

    pltpu.make_async_copy(got.at[0:119], got.at[0:119], pr_sem).wait()
    gather_ends(got, ends_s, z, w, left, right, turned)
    tile_products(left, right, turned, mask, valid, made, out_ref, out_sem)

    for b in range(4):
        pltpu.make_async_copy(made.at[b], out_ref.at[b], out_sem.at[b]).wait()
    pltpu.make_async_copy(got.at[0:119], got.at[0:119], ps_sem).wait()
    for c in range(2):
        for i in range(1, NX):
            raw_copy(c, i).wait_send()
            back_copy(c, xpeer(i)).wait_send()
        for i in range(NX):
            for d in range(2):
                if c == 0:
                    first_copy(d, xpeer(i)).wait_send()
                for h in range(1 + (c == 0), REACH + 1):
                    ring_copy(d, h, c, i).wait_send()


def body(raw, taps, pairs, counts):
    ends = pairs.reshape(128, 128, 2).transpose(0, 2, 1).reshape(256, 128)
    any_spec = pl.BlockSpec(memory_space=pl.ANY)
    vmem = pl.BlockSpec(memory_space=pltpu.VMEM)
    dma = pltpu.SemaphoreType.DMA
    tiles = pltpu.VMEM((4, 1536, 128), BF16)
    result = pl.pallas_call(
        whole_kernel,
        out_shape=jax.ShapeDtypeStruct((4, BR, 2, 1536), F32),
        in_specs=[any_spec] * 5,
        out_specs=any_spec,
        scratch_shapes=[
            pltpu.SMEM((33,), F32),
            pltpu.VMEM((256, 128), jnp.int32),
            pltpu.VMEM((1, 128), jnp.int32),
            pltpu.VMEM((4096, 512), F32),
            pltpu.VMEM((2, 4, 1024, 512), BF16),
            pltpu.VMEM((2, NX, CROWS, 1024), BF16),
            pltpu.VMEM((2, 2, 256, 256), BF16),
            pltpu.VMEM((2, 256, 256), BF16),
            pltpu.VMEM((17, CROWS, 256), F32),
            pltpu.VMEM((2, 17, CROWS, 256), BF16),
            pltpu.VMEM((4, 4 * BLK, 128), F32),
            pltpu.VMEM((2, 4, 4, BLK, 128), BF16),
            pltpu.VMEM((16, 128), jnp.int32),
            pltpu.SMEM((16, 128), jnp.int32),
            pltpu.SMEM((16, 128), jnp.int32),
            pltpu.VMEM((9, PLANE, BLK, 128), BF16),
            pltpu.VMEM((2, REACH, PLANE, BLK, 128), BF16),
            pltpu.VMEM((NZ * PLANE, BLK, 128), BF16),
            tiles, tiles, tiles,
            pltpu.VMEM((3, 144, 128), F32),
            pltpu.VMEM((8, 1536), F32),
            pltpu.VMEM((4, BR, 2, 1536), F32),
        ]
        + [pltpu.VMEM((32, BLK, 128), BF16)] * 9
        + [
            dma, dma((2,)), dma((2, 3)), dma((2, 3)), dma((2, 4)), dma((2, 4)),
            dma((2, 4, 8)), dma((2, 4, 8)), dma, dma, dma((5,)), dma((4,)),
        ],
        compiler_params=pltpu.CompilerParams(
            collective_id=0, has_side_effects=True, vmem_limit_bytes=60 << 20
        ),
        name="cross_spectra",
    )(raw, taps, ends, counts.reshape(1, 128), jnp.asarray(dft_tables()))
    return result.transpose(0, 2, 1, 3)


def solution(mesh):
    return jax.shard_map(
        body,
        mesh=mesh,
        in_specs=(P("sta", "sec"), P(), P(), P("sta")),
        out_specs=P("sec", None, None, "sta"),
        check_vma=False,
    )
```

```python
import functools
import math

import jax
import jax.numpy as jnp
import numpy as np
from jax import lax
from jax.experimental import pallas as pl
from jax.experimental.pallas import tpu as pltpu
from jax.sharding import PartitionSpec as P

MESH = pl.DeviceIdType.MESH
L = 4096
F = 1024
LOWBIN = 4
WB = 64
FH = 16
NH = 32
BR = 12
PLANE = 8
NZ = 16
NX = 4
REACH = 4
CROWS = 48
BLK = 4 * BR
F32 = jnp.float32
BF16 = jnp.bfloat16


def dft_tables():
    cols = np.arange(512)
    sect, part, band, mm = cols // 128, (cols // 64) % 2, (cols // 16) % 4, cols % 16
    m = (4 * sect + band) * 16 + mm + 1
    t = np.arange(1024)
    planes = []
    for r in (0, 2, 1, 3):
        angle = 2.0 * np.pi / L * ((t[:, None] * (4 * m + r)[None, :]) % L)
        planes.append(np.where(part[None, :] == 0, np.cos(angle), -np.sin(angle)))
    return np.concatenate(planes).astype(np.float32)


def split(value):
    high = value.astype(BF16)
    return high, (value - high.astype(F32)).astype(BF16)


def mm(a, b):
    return jnp.dot(a, b, preferred_element_type=F32)


def build_filters(taps_ref, toep_ref, box_ref):
    def rows(i, carry):
        start = pl.multiple_of(32 * i, 32)
        diff = (
            lax.broadcasted_iota(jnp.int32, (32, 256), 0)
            + 32 * i
            - lax.broadcasted_iota(jnp.int32, (32, 256), 1)
        )
        first = jnp.zeros((32, 256), F32)
        second = jnp.zeros((32, 256), F32)
        for k in range(2 * FH + 1):
            tap = taps_ref[k]
            first = jnp.where(diff == k + 112, tap, first)
            second = jnp.where(diff == k - 144, tap, second)
        for which, value in enumerate((first, second)):
            high, low = split(value)
            toep_ref[which, 0, pl.ds(start, 32)] = high
            toep_ref[which, 1, pl.ds(start, 32)] = low
        box_ref[0, pl.ds(start, 32)] = jnp.where(jnp.abs(diff - 128) <= NH, 1.0, 0.0).astype(BF16)
        box_ref[1, pl.ds(start, 32)] = jnp.where(jnp.abs(diff + 128) <= NH, 1.0, 0.0).astype(BF16)
        return carry

    lax.fori_loop(0, 8, rows, 0)


def split_tables(wide, tab_ref):
    def rows(i, carry):
        start = pl.multiple_of(32 * i, 32)
        for r in range(4):
            high, low = split(wide[pl.ds(1024 * r + start, 32)])
            tab_ref[0, r, pl.ds(start, 32)] = high
            tab_ref[1, r, pl.ds(start, 32)] = low
        return carry

    lax.fori_loop(0, 32, rows, 0)


def normalize(xin, toep_ref, box_ref, filt, mag):
    n = CROWS
    zero = jnp.zeros((n, 256), BF16)
    parts = [xin[q, :, 256 * k : 256 * k + 256] for q in range(4) for k in range(4)]
    x0 = jnp.concatenate([zero] + parts, axis=0)
    x1 = jnp.concatenate(parts + [zero], axis=0)
    filtered = (mm(x0, toep_ref[0, 0]) + mm(x1, toep_ref[1, 0])) + (
        mm(x0, toep_ref[0, 1]) + mm(x1, toep_ref[1, 1])
    )
    filt[...] = filtered.reshape(17, n, 256)
    high, low = split(jnp.abs(filtered))
    mag[0] = high.reshape(17, n, 256)
    mag[1] = low.reshape(17, n, 256)
    level = (
        mm(mag[0, 0:16].reshape(16 * n, 256), box_ref[0])
        + mm(mag[0, 1:17].reshape(16 * n, 256), box_ref[1])
    ) + (
        mm(mag[1, 0:16].reshape(16 * n, 256), box_ref[0])
        + mm(mag[1, 1:17].reshape(16 * n, 256), box_ref[1])
    )
    center = jnp.concatenate([filt[0:16, :, 128:256], filt[1:17, :, 0:128]], axis=-1)
    return center / (level.reshape(16, n, 256) * (1.0 / (2 * NH + 1)) + 1e-05)


def combine_quarters(normed):
    n = CROWS
    seg = normed.reshape(4, 4, n, 256)
    even, odd = seg[0] + seg[2], seg[1] + seg[3]
    flat = lambda v: jnp.concatenate([v[k] for k in range(4)], axis=-1)
    rows = [flat(even + odd), flat(even - odd)]
    rows += [jnp.concatenate([flat(seg[0] - seg[2]), flat(seg[1] - seg[3])], axis=0)]
    return [jnp.concatenate(split(value), axis=0) for value in rows]


def spectra_of(parts, tab_ref, half):
    n = CROWS
    cols = pl.ds(pl.multiple_of(256 * half, 256), 256)

    def transform(both, r):
        rows = both.shape[0] // 2
        full = mm(both, tab_ref[0, r, :, cols])
        return full[:rows] + full[rows:] + mm(both[:rows], tab_ref[1, r, :, cols])

    s0, s2 = transform(parts[0], 0), transform(parts[1], 1)
    odd1, odd3 = transform(parts[2], 2), transform(parts[2], 3)
    lane = lax.broadcasted_iota(jnp.int32, (n, 256), 1)
    sign = jnp.where((lane // 64) % 2 == 0, 1.0, -1.0)

    def swap(value):
        return jnp.concatenate(
            [pltpu.roll(value[:, 128 * s : 128 * s + 128], 64, 1) for s in range(2)], axis=-1
        )

    s1 = odd1[:n] + sign * swap(odd1[n:])
    s3 = odd3[:n] - sign * swap(odd3[n:])
    return s0, s1, s2, s3


def whiten(spectra, stage, out_ref, half):
    n = CROWS
    power = sum(s * s for s in spectra)
    li = lax.broadcasted_iota(jnp.int32, (128, 128), 0)
    lj = lax.broadcasted_iota(jnp.int32, (128, 128), 1)
    group = jnp.where((li // 16) % 4 == (lj // 16) % 4, 1.0, 0.0).astype(BF16)
    tall = jnp.concatenate([power[:, 128 * s : 128 * s + 128] for s in range(2)], axis=0)
    high, low = split(tall)
    band = mm(high, group) + mm(low, group)
    scale = lax.rsqrt(band * (1.0 / WB) + 1e-06)
    slot = (lax.broadcasted_iota(jnp.int32, (n, 128), 1) // 16) % 4
    for s in range(2):
        sc = scale[n * s : n * s + n]
        parts = [spectra[r][:, 128 * s : 128 * s + 128] * sc for r in range(4)]
        for b in range(4):
            value = None
            for r in range(4):
                moved = parts[r] if r == b else pltpu.roll(parts[r], (16 * (r - b)) % 128, 1)
                value = moved if value is None else jnp.where(slot == r, moved, value)
            for k in range(4):
                stage[s, BLK * k + BR * b : BLK * k + BR * b + BR, :] = value[BR * k : BR * k + BR]
        out_ref[2 * half + s] = stage[s].astype(BF16).reshape(4, BLK, 128)


def column_masks(count_ref, mask_ref, valid_ref):
    row = (lax.broadcasted_iota(jnp.int32, (144, 128), 0) * 10923) >> 17
    lane = lax.broadcasted_iota(jnp.int32, (144, 128), 1)
    for cg in range(3):
        column = ((lane + 128 * cg) * 10923) >> 17
        mask_ref[cg] = jnp.where(row + 2 * (128 * cg // 24) == column, 1.0, 0.0)
    tile = lax.broadcasted_iota(jnp.int32, (128, 1536), 0)
    column = lax.broadcasted_iota(jnp.int32, (128, 1536), 1)
    offset = column - BR * tile
    spread = jnp.where((offset >= 0) & (offset < BR), 1.0, 0.0).astype(BF16)
    counts = jnp.broadcast_to(count_ref[...].astype(F32), (8, 128)).astype(BF16)
    column = lax.broadcasted_iota(jnp.int32, (8, 1536), 1)
    station = ((column - BR * ((column * 10923) >> 17)) * 10923) >> 15
    valid_ref[...] = jnp.where(station.astype(F32) < mm(counts, spread), 1.0 / WB, 0.0)


def gather_ends(got, ends, z, w, left, right, turned):
    sign = jnp.where(lax.broadcasted_iota(jnp.int32, (BLK, 128), 1) < 64, -1.0, 1.0)

    def place(end):
        step = ((end >> 8) - z) & (NZ - 1)
        order = jnp.where(step < NZ // 2, 2 * step, 2 * NZ - 1 - 2 * step)
        return ((end >> 5) & (PLANE - 1)) * NZ + order

    def four(g, carry):
        rows = pl.ds(pl.multiple_of(BLK * g, 16), BLK)
        for e in range(2):
            tiles = [got[place(ends[2 * w + e, 4 * g + k])].astype(F32) for k in range(4)]
            for b in range(4):
                value = jnp.concatenate([t[BR * b : BR * b + BR] for t in tiles], axis=0)
                if e == 0:
                    left[b, rows] = value.astype(BF16)
                else:
                    right[b, rows] = value.astype(BF16)
                    turned[b, rows] = (sign * pltpu.roll(value, 64, 1)).astype(BF16)
        return carry

    lax.fori_loop(0, 32, four, 0, unroll=8)


def tile_products(left, right, turned, mask_ref, valid_ref, made, out_ref, out_sem):
    for b in range(4):
        for cg in range(12):
            first = 2 * (128 * cg // 24)
            rows = left[b, BR * first : BR * first + 144]
            cols = slice(128 * cg, 128 * cg + 128)
            other = jnp.concatenate([right[b, cols], turned[b, cols]], axis=0)
            full = lax.dot_general(
                rows, other, (((1,), (1,)), ((), ())), preferred_element_type=F32
            )
            total = jnp.zeros((24, 256), F32)
            for k in range(6):
                keep = mask_ref[cg % 3, 24 * k : 24 * k + 24]
                total += jnp.concatenate([keep, keep], axis=1) * full[24 * k : 24 * k + 24]
            short = total[:BR] + total[BR:]
            valid = valid_ref[0:1, cols]
            made[b, :, 0, cols] = short[:, :128] * valid
            made[b, :, 1, cols] = short[:, 128:] * valid
        pltpu.make_async_copy(made.at[b], out_ref.at[b], out_sem.at[b]).start()


def whole_kernel(
    raw_ref, taps_hbm, ends_hbm, count_hbm, tab_hbm, out_ref,
    taps_ref, ends_ref, count_ref, wide, tab, xin, toep, box, filt, mag, stage, wsend, pick_v, pick_s, ends_s,
    near_stage, far_stage, got, left, right, turned, mask, valid, made,
    slot0, slot1, slot2, slot3, slot4, slot5, slot6, slot7, slot8,
    tab_sem, own_sem, xs_sem, xr_sem, bs_sem, br_sem, zs_sem, zr_sem,
    ps_sem, pr_sem, pk_sem, out_sem,
):
    slots = (slot0, slot1, slot2, slot3, slot4, slot5, slot6, slot7, slot8)
    sta = lax.axis_index("sta")
    x = lax.axis_index("sec")
    z = sta // PLANE
    w = sta % PLANE

    def at(step, ww):
        return ((z + step + NZ) % NZ) * PLANE + ww

    def xpeer(i):
        return (x + i) % NX

    def from_x(i):
        return (x + NX - i) % NX

    barrier = pltpu.get_barrier_semaphore()

    def greet(peer):
        pl.semaphore_signal(barrier, inc=1, device_id=peer, device_id_type=MESH)

    for i in range(1, NX):
        greet((sta, xpeer(i)))
    greet((at(1, w), x))
    greet((at(-1, w), x))
    for i in range(1, PLANE):
        greet((at(0, (w + i) % PLANE), x))

    taps_copy = pltpu.make_async_copy(taps_hbm, taps_ref, pk_sem.at[2])
    taps_copy.start()
    all_ends_copy = pltpu.make_async_copy(ends_hbm, ends_ref, pk_sem.at[3])
    all_ends_copy.start()
    count_copy = pltpu.make_async_copy(count_hbm, count_ref, pk_sem.at[4])
    count_copy.start()
    tab_copy = pltpu.make_async_copy(tab_hbm, wide, tab_sem)
    ends_copy = pltpu.make_async_copy(
        ends_hbm.at[pl.ds(pl.multiple_of(16 * z, 16), 16)], ends_s, pk_sem.at[0]
    )
    ends_copy.start()

    def raw_rows(q, c):
        return raw_ref.at[pl.ds(pl.multiple_of(96 * q + CROWS * c, 16), CROWS)]

    def own_copy(c):
        return pltpu.make_async_copy(raw_rows(x, c), xin.at[c, x], own_sem.at[c])

    for c in range(2):
        own_copy(c).start()
    pl.semaphore_wait(barrier, NX - 1 + 2 + PLANE - 1)

    def raw_copy(c, i):
        return pltpu.make_async_remote_copy(
            src_ref=raw_rows(xpeer(i), c),
            dst_ref=xin.at[c, x],
            send_sem=xs_sem.at[c, i - 1],
            recv_sem=xr_sem.at[c, i - 1],
            device_id=(sta, xpeer(i)),
            device_id_type=MESH,
        )

    def raw_start(c):
        for i in (2, 1, 3):
            raw_copy(c, i).start()

    def raw_wait(c):
        own_copy(c).wait()
        for i in range(1, NX):
            dst = xin.at[c, from_x(i)]
            pltpu.make_async_copy(dst, dst, xr_sem.at[c, i - 1]).wait()

    raw_start(0)
    tab_copy.start()

    taps_copy.wait()
    build_filters(taps_ref, toep, box)
    all_ends_copy.wait()
    lane = lax.broadcasted_iota(jnp.int32, (16, 128), 1)
    picks = jnp.zeros((16, 128), jnp.int32)

    def asked(step, source):
        rows = ends_ref[pl.ds(pl.multiple_of(16 * ((z + step + NZ) % NZ), 16), 16), :]
        return jnp.max(jnp.where(rows // 32 == source, rows % 32, 0), axis=1, keepdims=True)

    wanted = [(0, at(-s if s <= REACH else s - REACH, w)) for s in range(9)]
    wanted += [(h, at(-REACH, w)) for h in range(1, REACH + 1)]
    wanted += [(-h, at(REACH, w)) for h in range(1, REACH + 1)]
    for col, (step, source) in enumerate(wanted):
        picks = jnp.where(lane == col, asked(step, source), picks)
    pick_v[...] = picks
    pick_copy = pltpu.make_async_copy(pick_v, pick_s, pk_sem.at[1])
    pick_copy.start()
    count_copy.wait()
    column_masks(count_ref, mask, valid)
    raw_start(1)
    tab_copy.wait()
    split_tables(wide, tab)
    pick_copy.wait()
    ends_copy.wait()

    def back_copy(c, s):
        i = (s - x + NX) % NX
        return pltpu.make_async_remote_copy(
            src_ref=wsend.at[c, s],
            dst_ref=slot0.at[pl.ds(8 * x + 4 * c, 4)],
            send_sem=bs_sem.at[c, i],
            recv_sem=br_sem.at[c, i],
            device_id=(sta, s),
            device_id_type=MESH,
        )

    def first_copy(d, s):
        i = (s - x + NX) % NX
        return pltpu.make_async_remote_copy(
            src_ref=wsend.at[0, s],
            dst_ref=slots[1 + 4 * d].at[pl.ds(8 * x, 4)],
            send_sem=zs_sem.at[d, 0, i],
            recv_sem=zr_sem.at[d, 0, i],
            device_id=(at(1 - 2 * d, w), s),
            device_id_type=MESH,
        )

    def section_start(c, half):
        if c == 0:
            for s in (2 * half, 2 * half + 1):
                for d in range(2):
                    first_copy(d, s).start()
        for s in (2 * half, 2 * half + 1):

            @pl.when(s != x)
            def _():
                back_copy(c, s).start()

    def back_wait(c, i):
        rows = slot0.at[pl.ds(8 * from_x(i) + 4 * c, 4)]
        pltpu.make_async_copy(rows, rows, br_sem.at[c, i]).wait()

    def ring_wait(d, h, c, i):
        rows = slots[h + 4 * d].at[pl.ds(8 * from_x(i) + 4 * c, 4)]
        pltpu.make_async_copy(rows, rows, zr_sem.at[d, h - 1, 4 * c + i]).wait()

    def ring_copy(d, h, c, i):
        rows = pl.ds(8 * from_x(i) + 4 * c, 4)
        return pltpu.make_async_remote_copy(
            src_ref=(slots[0] if h == 1 else slots[h - 1 + 4 * d]).at[rows],
            dst_ref=slots[h + 4 * d].at[rows],
            send_sem=zs_sem.at[d, h - 1, 4 * c + i],
            recv_sem=zr_sem.at[d, h - 1, 4 * c + i],
            device_id=(at(1 - 2 * d, w), x),
            device_id_type=MESH,
        )

    def ring_start(h, c, i):
        for d in range(2):
            if h > 1:
                ring_wait(d, h - 1, c, i)
            ring_copy(d, h, c, i).start()

    def first_start(c):
        for i in range(1, NX):
            back_wait(c, i)
            ring_start(1, c, i)

    def asked_block(ww, col):
        return jnp.clip(jnp.maximum(pick_s[2 * ww, col], pick_s[2 * ww + 1, col]), 0, 31)

    def place_copy(source, place, step, ww):
        return pltpu.make_async_remote_copy(
            src_ref=source,
            dst_ref=got.at[w * NZ + place],
            send_sem=ps_sem,
            recv_sem=pr_sem,
            device_id=(at(step, ww), x),
            device_id_type=MESH,
        )

    def near_picks(s):
        place = 0 if s == 0 else (2 * s - 1 if s <= REACH else 2 * (s - REACH))

        def one(i, carry):
            ww = (w + i) % PLANE
            near_stage[s, i] = slots[s][asked_block(ww, s)]
            place_copy(near_stage.at[s, i], place, 0, ww).start()
            return carry

        lax.fori_loop(1, PLANE, one, 0)
        got[w * NZ + place] = slots[s][asked_block(w, s)]

    def far_picks(k):
        def one(i, carry):
            for d in range(2):
                ww = i if k < REACH else 2 * i + d
                place = 2 * (REACH + k) - 1 + (d if k < REACH else 0)
                far_stage[d, k - 1, i] = slots[REACH + 4 * d][asked_block(ww, 9 + 4 * d + k - 1)]
                place_copy(far_stage.at[d, k - 1, i], place, k * (1 - 2 * d), ww).start()
            return carry

        lax.fori_loop(0, PLANE if k < REACH else PLANE // 2, one, 0)

    mine = x // 2
    for c in range(2):
        raw_wait(c)
        parts = combine_quarters(normalize(xin.at[c], toep, box, filt, mag))
        whiten(spectra_of(parts, tab, mine), stage, wsend.at[c], mine)
        section_start(c, mine)
        slot0[pl.ds(8 * x + 4 * c, 4)] = wsend[c, x]
        if c == 1:
            ring_start(1, 1, 0)
            for i in range(NX):
                ring_start(2, 0, i)
        whiten(spectra_of(parts, tab, 1 - mine), stage, wsend.at[c], 1 - mine)
        section_start(c, 1 - mine)
    for i in range(1, NX):
        back_wait(0, i)
    first_start(1)
    for i in range(NX):
        ring_start(2, 1, i)
    near_picks(0)
    near_picks(1)
    near_picks(1 + REACH)
    for h in range(3, REACH + 1):
        for c in range(2):
            for i in range(NX):
                ring_start(h, c, i)
        near_picks(h - 1)
        near_picks(h - 1 + REACH)
    for c in range(2):
        for i in range(NX):
            for d in range(2):
                ring_wait(d, REACH, c, i)
    for k in range(1, REACH + 1):
        far_picks(k)
    near_picks(REACH)
    near_picks(2 * REACH)

    pltpu.make_async_copy(got.at[0:119], got.at[0:119], pr_sem).wait()
    gather_ends(got, ends_s, z, w, left, right, turned)
    tile_products(left, right, turned, mask, valid, made, out_ref, out_sem)

    for b in range(4):
        pltpu.make_async_copy(made.at[b], out_ref.at[b], out_sem.at[b]).wait()
    pltpu.make_async_copy(got.at[0:119], got.at[0:119], ps_sem).wait()
    for c in range(2):
        for i in range(1, NX):
            raw_copy(c, i).wait_send()
            back_copy(c, xpeer(i)).wait_send()
        for i in range(NX):
            for d in range(2):
                if c == 0:
                    first_copy(d, xpeer(i)).wait_send()
                for h in range(1 + (c == 0), REACH + 1):
                    ring_copy(d, h, c, i).wait_send()


def body(raw, taps, pairs, counts):
    ends = pairs.reshape(128, 128, 2).transpose(0, 2, 1).reshape(256, 128)
    any_spec = pl.BlockSpec(memory_space=pl.ANY)
    vmem = pl.BlockSpec(memory_space=pltpu.VMEM)
    dma = pltpu.SemaphoreType.DMA
    tiles = pltpu.VMEM((4, 1536, 128), BF16)
    result = pl.pallas_call(
        whole_kernel,
        out_shape=jax.ShapeDtypeStruct((4, BR, 2, 1536), F32),
        in_specs=[any_spec] * 5,
        out_specs=any_spec,
        scratch_shapes=[
            pltpu.SMEM((33,), F32),
            pltpu.VMEM((256, 128), jnp.int32),
            pltpu.VMEM((1, 128), jnp.int32),
            pltpu.VMEM((4096, 512), F32),
            pltpu.VMEM((2, 4, 1024, 512), BF16),
            pltpu.VMEM((2, NX, CROWS, 1024), BF16),
            pltpu.VMEM((2, 2, 256, 256), BF16),
            pltpu.VMEM((2, 256, 256), BF16),
            pltpu.VMEM((17, CROWS, 256), F32),
            pltpu.VMEM((2, 17, CROWS, 256), BF16),
            pltpu.VMEM((4, 4 * BLK, 128), F32),
            pltpu.VMEM((2, 4, 4, BLK, 128), BF16),
            pltpu.VMEM((16, 128), jnp.int32),
            pltpu.SMEM((16, 128), jnp.int32),
            pltpu.SMEM((16, 128), jnp.int32),
            pltpu.VMEM((9, PLANE, BLK, 128), BF16),
            pltpu.VMEM((2, REACH, PLANE, BLK, 128), BF16),
            pltpu.VMEM((NZ * PLANE, BLK, 128), BF16),
            tiles, tiles, tiles,
            pltpu.VMEM((3, 144, 128), F32),
            pltpu.VMEM((8, 1536), F32),
            pltpu.VMEM((4, BR, 2, 1536), F32),
        ]
        + [pltpu.VMEM((32, BLK, 128), BF16)] * 9
        + [
            dma, dma((2,)), dma((2, 3)), dma((2, 3)), dma((2, 4)), dma((2, 4)),
            dma((2, 4, 8)), dma((2, 4, 8)), dma, dma, dma((5,)), dma((4,)),
        ],
        compiler_params=pltpu.CompilerParams(
            collective_id=0, has_side_effects=True, vmem_limit_bytes=60 << 20
        ),
        name="cross_spectra",
    )(raw, taps, ends, counts.reshape(1, 128), jnp.asarray(dft_tables()))
    return result.transpose(0, 2, 1, 3)


def solution(mesh):
    return jax.shard_map(
        body,
        mesh=mesh,
        in_specs=(P("sta", "sec"), P(), P(), P("sta")),
        out_specs=P("sec", None, None, "sta"),
        check_vma=False,
    )
```

```python
import functools
import math

import jax
import jax.numpy as jnp
import numpy as np
from jax import lax
from jax.experimental import pallas as pl
from jax.experimental.pallas import tpu as pltpu
from jax.sharding import PartitionSpec as P

MESH = pl.DeviceIdType.MESH
L = 4096
F = 1024
LOWBIN = 4
WB = 64
FH = 16
NH = 32
BR = 12
PLANE = 8
NZ = 16
NX = 4
REACH = 4
CROWS = 48
BLK = 4 * BR
F32 = jnp.float32
BF16 = jnp.bfloat16


def dft_tables():
    cols = np.arange(512)
    sect, part, band, mm = cols // 128, (cols // 64) % 2, (cols // 16) % 4, cols % 16
    m = (4 * sect + band) * 16 + mm + 1
    t = np.arange(1024)
    planes = []
    for r in (0, 2, 1, 3):
        angle = 2.0 * np.pi / L * ((t[:, None] * (4 * m + r)[None, :]) % L)
        planes.append(np.where(part[None, :] == 0, np.cos(angle), -np.sin(angle)))
    return np.concatenate(planes).astype(np.float32)


def split(value):
    high = value.astype(BF16)
    return high, (value - high.astype(F32)).astype(BF16)


def mm(a, b):
    return jnp.dot(a, b, preferred_element_type=F32)


def build_filters(taps_ref, toep_ref, box_ref):
    def rows(i, carry):
        start = pl.multiple_of(32 * i, 32)
        diff = (
            lax.broadcasted_iota(jnp.int32, (32, 256), 0)
            + 32 * i
            - lax.broadcasted_iota(jnp.int32, (32, 256), 1)
        )
        first = jnp.zeros((32, 256), F32)
        second = jnp.zeros((32, 256), F32)
        for k in range(2 * FH + 1):
            tap = taps_ref[k]
            first = jnp.where(diff == k + 112, tap, first)
            second = jnp.where(diff == k - 144, tap, second)
        for which, value in enumerate((first, second)):
            high, low = split(value)
            toep_ref[which, 0, pl.ds(start, 32)] = high
            toep_ref[which, 1, pl.ds(start, 32)] = low
        box_ref[0, pl.ds(start, 32)] = jnp.where(jnp.abs(diff - 128) <= NH, 1.0, 0.0).astype(BF16)
        box_ref[1, pl.ds(start, 32)] = jnp.where(jnp.abs(diff + 128) <= NH, 1.0, 0.0).astype(BF16)
        return carry

    lax.fori_loop(0, 8, rows, 0)


def split_tables(wide, tab_ref):
    def rows(i, carry):
        start = pl.multiple_of(32 * i, 32)
        for r in range(4):
            high, low = split(wide[pl.ds(1024 * r + start, 32)])
            tab_ref[0, r, pl.ds(start, 32)] = high
            tab_ref[1, r, pl.ds(start, 32)] = low
        return carry

    lax.fori_loop(0, 32, rows, 0)


def normalize(xin, toep_ref, box_ref, filt, mag):
    n = CROWS
    zero = jnp.zeros((n, 256), BF16)
    parts = [xin[q, :, 256 * k : 256 * k + 256] for q in range(4) for k in range(4)]
    x0 = jnp.concatenate([zero] + parts, axis=0)
    x1 = jnp.concatenate(parts + [zero], axis=0)
    filtered = (mm(x0, toep_ref[0, 0]) + mm(x1, toep_ref[1, 0])) + (
        mm(x0, toep_ref[0, 1]) + mm(x1, toep_ref[1, 1])
    )
    filt[...] = filtered.reshape(17, n, 256)
    high, low = split(jnp.abs(filtered))
    mag[0] = high.reshape(17, n, 256)
    mag[1] = low.reshape(17, n, 256)
    level = (
        mm(mag[0, 0:16].reshape(16 * n, 256), box_ref[0])
        + mm(mag[0, 1:17].reshape(16 * n, 256), box_ref[1])
    ) + (
        mm(mag[1, 0:16].reshape(16 * n, 256), box_ref[0])
        + mm(mag[1, 1:17].reshape(16 * n, 256), box_ref[1])
    )
    center = jnp.concatenate([filt[0:16, :, 128:256], filt[1:17, :, 0:128]], axis=-1)
    return center / (level.reshape(16, n, 256) * (1.0 / (2 * NH + 1)) + 1e-05)


def combine_quarters(normed):
    n = CROWS
    seg = normed.reshape(4, 4, n, 256)
    even, odd = seg[0] + seg[2], seg[1] + seg[3]
    flat = lambda v: jnp.concatenate([v[k] for k in range(4)], axis=-1)
    rows = [flat(even + odd), flat(even - odd)]
    rows += [jnp.concatenate([flat(seg[0] - seg[2]), flat(seg[1] - seg[3])], axis=0)]
    return [jnp.concatenate(split(value), axis=0) for value in rows]


def spectra_of(parts, tab_ref, half):
    n = CROWS
    cols = pl.ds(pl.multiple_of(256 * half, 256), 256)

    def transform(both, r):
        rows = both.shape[0] // 2
        full = mm(both, tab_ref[0, r, :, cols])
        return full[:rows] + full[rows:] + mm(both[:rows], tab_ref[1, r, :, cols])

    s0, s2 = transform(parts[0], 0), transform(parts[1], 1)
    odd1, odd3 = transform(parts[2], 2), transform(parts[2], 3)
    lane = lax.broadcasted_iota(jnp.int32, (n, 256), 1)
    sign = jnp.where((lane // 64) % 2 == 0, 1.0, -1.0)

    def swap(value):
        return jnp.concatenate(
            [pltpu.roll(value[:, 128 * s : 128 * s + 128], 64, 1) for s in range(2)], axis=-1
        )

    s1 = odd1[:n] + sign * swap(odd1[n:])
    s3 = odd3[:n] - sign * swap(odd3[n:])
    return s0, s1, s2, s3


def whiten(spectra, stage, out_ref, half):
    n = CROWS
    power = sum(s * s for s in spectra)
    li = lax.broadcasted_iota(jnp.int32, (128, 128), 0)
    lj = lax.broadcasted_iota(jnp.int32, (128, 128), 1)
    group = jnp.where((li // 16) % 4 == (lj // 16) % 4, 1.0, 0.0).astype(BF16)
    tall = jnp.concatenate([power[:, 128 * s : 128 * s + 128] for s in range(2)], axis=0)
    high, low = split(tall)
    band = mm(high, group) + mm(low, group)
    scale = lax.rsqrt(band * (1.0 / WB) + 1e-06)
    slot = (lax.broadcasted_iota(jnp.int32, (n, 128), 1) // 16) % 4
    for s in range(2):
        sc = scale[n * s : n * s + n]
        parts = [spectra[r][:, 128 * s : 128 * s + 128] * sc for r in range(4)]
        for b in range(4):
            value = None
            for r in range(4):
                moved = parts[r] if r == b else pltpu.roll(parts[r], (16 * (r - b)) % 128, 1)
                value = moved if value is None else jnp.where(slot == r, moved, value)
            for k in range(4):
                stage[s, BLK * k + BR * b : BLK * k + BR * b + BR, :] = value[BR * k : BR * k + BR]
        out_ref[2 * half + s] = stage[s].astype(BF16).reshape(4, BLK, 128)


def column_masks(count_ref, mask_ref, valid_ref):
    row = (lax.broadcasted_iota(jnp.int32, (144, 128), 0) * 10923) >> 17
    lane = lax.broadcasted_iota(jnp.int32, (144, 128), 1)
    for cg in range(3):
        column = ((lane + 128 * cg) * 10923) >> 17
        mask_ref[cg] = jnp.where(row + 2 * (128 * cg // 24) == column, 1.0, 0.0)
    tile = lax.broadcasted_iota(jnp.int32, (128, 1536), 0)
    column = lax.broadcasted_iota(jnp.int32, (128, 1536), 1)
    offset = column - BR * tile
    spread = jnp.where((offset >= 0) & (offset < BR), 1.0, 0.0).astype(BF16)
    counts = jnp.broadcast_to(count_ref[...].astype(F32), (8, 128)).astype(BF16)
    column = lax.broadcasted_iota(jnp.int32, (8, 1536), 1)
    station = ((column - BR * ((column * 10923) >> 17)) * 10923) >> 15
    valid_ref[...] = jnp.where(station.astype(F32) < mm(counts, spread), 1.0 / WB, 0.0)


def gather_ends(got, ends, z, w, left, right, turned):
    sign = jnp.where(lax.broadcasted_iota(jnp.int32, (BLK, 128), 1) < 64, -1.0, 1.0)

    def place(end):
        step = ((end >> 8) - z) & (NZ - 1)
        order = jnp.where(step < NZ // 2, 2 * step, 2 * NZ - 1 - 2 * step)
        return ((end >> 5) & (PLANE - 1)) * NZ + order

    def four(g, carry):
        rows = pl.ds(pl.multiple_of(BLK * g, 16), BLK)
        for e in range(2):
            tiles = [got[place(ends[2 * w + e, 4 * g + k])].astype(F32) for k in range(4)]
            for b in range(4):
                value = jnp.concatenate([t[BR * b : BR * b + BR] for t in tiles], axis=0)
                if e == 0:
                    left[b, rows] = value.astype(BF16)
                else:
                    right[b, rows] = value.astype(BF16)
                    turned[b, rows] = (sign * pltpu.roll(value, 64, 1)).astype(BF16)
        return carry

    lax.fori_loop(0, 32, four, 0, unroll=16)


def tile_products(left, right, turned, mask_ref, valid_ref, made, out_ref, out_sem):
    for b in range(4):
        for cg in range(12):
            first = 2 * (128 * cg // 24)
            rows = left[b, BR * first : BR * first + 144]
            cols = slice(128 * cg, 128 * cg + 128)
            other = jnp.concatenate([right[b, cols], turned[b, cols]], axis=0)
            full = lax.dot_general(
                rows, other, (((1,), (1,)), ((), ())), preferred_element_type=F32
            )
            total = jnp.zeros((24, 256), F32)
            for k in range(6):
                keep = mask_ref[cg % 3, 24 * k : 24 * k + 24]
                total += jnp.concatenate([keep, keep], axis=1) * full[24 * k : 24 * k + 24]
            short = total[:BR] + total[BR:]
            valid = valid_ref[0:1, cols]
            made[b, :, 0, cols] = short[:, :128] * valid
            made[b, :, 1, cols] = short[:, 128:] * valid
        pltpu.make_async_copy(made.at[b], out_ref.at[b], out_sem.at[b]).start()


def whole_kernel(
    raw_ref, taps_hbm, ends_hbm, count_hbm, tab_hbm, out_ref,
    taps_ref, ends_ref, count_ref, wide, tab, xin, toep, box, filt, mag, stage, wsend, pick_v, pick_s, ends_s,
    near_stage, far_stage, got, left, right, turned, mask, valid, made,
    slot0, slot1, slot2, slot3, slot4, slot5, slot6, slot7, slot8,
    tab_sem, own_sem, xs_sem, xr_sem, bs_sem, br_sem, zs_sem, zr_sem,
    ps_sem, pr_sem, pk_sem, out_sem,
):
    slots = (slot0, slot1, slot2, slot3, slot4, slot5, slot6, slot7, slot8)
    sta = lax.axis_index("sta")
    x = lax.axis_index("sec")
    z = sta // PLANE
    w = sta % PLANE

    def at(step, ww):
        return ((z + step + NZ) % NZ) * PLANE + ww

    def xpeer(i):
        return (x + i) % NX

    def from_x(i):
        return (x + NX - i) % NX

    barrier = pltpu.get_barrier_semaphore()

    def greet(peer):
        pl.semaphore_signal(barrier, inc=1, device_id=peer, device_id_type=MESH)

    for i in range(1, NX):
        greet((sta, xpeer(i)))
    greet((at(1, w), x))
    greet((at(-1, w), x))
    for i in range(1, PLANE):
        greet((at(0, (w + i) % PLANE), x))

    taps_copy = pltpu.make_async_copy(taps_hbm, taps_ref, pk_sem.at[2])
    taps_copy.start()
    all_ends_copy = pltpu.make_async_copy(ends_hbm, ends_ref, pk_sem.at[3])
    all_ends_copy.start()
    count_copy = pltpu.make_async_copy(count_hbm, count_ref, pk_sem.at[4])
    count_copy.start()
    tab_copy = pltpu.make_async_copy(tab_hbm, wide, tab_sem)
    ends_copy = pltpu.make_async_copy(
        ends_hbm.at[pl.ds(pl.multiple_of(16 * z, 16), 16)], ends_s, pk_sem.at[0]
    )
    ends_copy.start()

    def raw_rows(q, c):
        return raw_ref.at[pl.ds(pl.multiple_of(96 * q + CROWS * c, 16), CROWS)]

    def own_copy(c):
        return pltpu.make_async_copy(raw_rows(x, c), xin.at[c, x], own_sem.at[c])

    for c in range(2):
        own_copy(c).start()
    pl.semaphore_wait(barrier, NX - 1 + 2 + PLANE - 1)

    def raw_copy(c, i):
        return pltpu.make_async_remote_copy(
            src_ref=raw_rows(xpeer(i), c),
            dst_ref=xin.at[c, x],
            send_sem=xs_sem.at[c, i - 1],
            recv_sem=xr_sem.at[c, i - 1],
            device_id=(sta, xpeer(i)),
            device_id_type=MESH,
        )

    def raw_start(c):
        for i in (2, 1, 3):
            if c == 1:
                raw_copy(c, i).start()
                continue
            for part in range(3):
                pltpu.make_async_remote_copy(
                    src_ref=raw_ref.at[pl.ds(pl.multiple_of(96 * xpeer(i) + 16 * part, 16), 16)],
                    dst_ref=xin.at[0, x, 16 * part : 16 * part + 16],
                    send_sem=xs_sem.at[0, i - 1],
                    recv_sem=xr_sem.at[0, i - 1],
                    device_id=(sta, xpeer(i)),
                    device_id_type=MESH,
                ).start()

    def raw_wait(c):
        own_copy(c).wait()
        for i in range(1, NX):
            dst = xin.at[c, from_x(i)]
            pltpu.make_async_copy(dst, dst, xr_sem.at[c, i - 1]).wait()

    raw_start(0)
    raw_start(1)
    tab_copy.start()

    taps_copy.wait()
    build_filters(taps_ref, toep, box)
    all_ends_copy.wait()
    lane = lax.broadcasted_iota(jnp.int32, (16, 128), 1)
    picks = jnp.zeros((16, 128), jnp.int32)

    def asked(step, source):
        rows = ends_ref[pl.ds(pl.multiple_of(16 * ((z + step + NZ) % NZ), 16), 16), :]
        return jnp.max(jnp.where(rows // 32 == source, rows % 32, 0), axis=1, keepdims=True)

    wanted = [(0, at(-s if s <= REACH else s - REACH, w)) for s in range(9)]
    wanted += [(h, at(-REACH, w)) for h in range(1, REACH + 1)]
    wanted += [(-h, at(REACH, w)) for h in range(1, REACH + 1)]
    for col, (step, source) in enumerate(wanted):
        picks = jnp.where(lane == col, asked(step, source), picks)
    pick_v[...] = picks
    pick_copy = pltpu.make_async_copy(pick_v, pick_s, pk_sem.at[1])
    pick_copy.start()
    count_copy.wait()
    column_masks(count_ref, mask, valid)
    tab_copy.wait()
    split_tables(wide, tab)
    pick_copy.wait()
    ends_copy.wait()

    def back_copy(c, s):
        i = (s - x + NX) % NX
        return pltpu.make_async_remote_copy(
            src_ref=wsend.at[c, s],
            dst_ref=slot0.at[pl.ds(8 * x + 4 * c, 4)],
            send_sem=bs_sem.at[c, i],
            recv_sem=br_sem.at[c, i],
            device_id=(sta, s),
            device_id_type=MESH,
        )

    def first_copy(d, s):
        i = (s - x + NX) % NX
        return pltpu.make_async_remote_copy(
            src_ref=wsend.at[0, s],
            dst_ref=slots[1 + 4 * d].at[pl.ds(8 * x, 4)],
            send_sem=zs_sem.at[d, 0, i],
            recv_sem=zr_sem.at[d, 0, i],
            device_id=(at(1 - 2 * d, w), s),
            device_id_type=MESH,
        )

    def section_start(c, half):
        if c == 0:
            for s in (2 * half, 2 * half + 1):
                for d in range(2):
                    first_copy(d, s).start()
        for s in (2 * half, 2 * half + 1):

            @pl.when(s != x)
            def _():
                back_copy(c, s).start()

    def back_wait(c, i):
        rows = slot0.at[pl.ds(8 * from_x(i) + 4 * c, 4)]
        pltpu.make_async_copy(rows, rows, br_sem.at[c, i]).wait()

    def ring_wait(d, h, c, i):
        rows = slots[h + 4 * d].at[pl.ds(8 * from_x(i) + 4 * c, 4)]
        pltpu.make_async_copy(rows, rows, zr_sem.at[d, h - 1, 4 * c + i]).wait()

    def ring_copy(d, h, c, i):
        rows = pl.ds(8 * from_x(i) + 4 * c, 4)
        return pltpu.make_async_remote_copy(
            src_ref=(slots[0] if h == 1 else slots[h - 1 + 4 * d]).at[rows],
            dst_ref=slots[h + 4 * d].at[rows],
            send_sem=zs_sem.at[d, h - 1, 4 * c + i],
            recv_sem=zr_sem.at[d, h - 1, 4 * c + i],
            device_id=(at(1 - 2 * d, w), x),
            device_id_type=MESH,
        )

    def ring_start(h, c, i):
        for d in range(2):
            if h > 1:
                ring_wait(d, h - 1, c, i)
            ring_copy(d, h, c, i).start()

    def first_start(c):
        for i in range(1, NX):
            back_wait(c, i)
            ring_start(1, c, i)

    def asked_block(ww, col):
        return jnp.clip(jnp.maximum(pick_s[2 * ww, col], pick_s[2 * ww + 1, col]), 0, 31)

    def place_copy(source, place, step, ww):
        return pltpu.make_async_remote_copy(
            src_ref=source,
            dst_ref=got.at[w * NZ + place],
            send_sem=ps_sem,
            recv_sem=pr_sem,
            device_id=(at(step, ww), x),
            device_id_type=MESH,
        )

    def near_picks(s):
        place = 0 if s == 0 else (2 * s - 1 if s <= REACH else 2 * (s - REACH))

        def one(i, carry):
            ww = (w + i) % PLANE
            near_stage[s, i] = slots[s][asked_block(ww, s)]
            place_copy(near_stage.at[s, i], place, 0, ww).start()
            return carry

        lax.fori_loop(1, PLANE, one, 0)
        got[w * NZ + place] = slots[s][asked_block(w, s)]

    def far_picks(k):
        def one(i, carry):
            for d in range(2):
                ww = i if k < REACH else 2 * i + d
                place = 2 * (REACH + k) - 1 + (d if k < REACH else 0)
                far_stage[d, k - 1, i] = slots[REACH + 4 * d][asked_block(ww, 9 + 4 * d + k - 1)]
                place_copy(far_stage.at[d, k - 1, i], place, k * (1 - 2 * d), ww).start()
            return carry

        lax.fori_loop(0, PLANE if k < REACH else PLANE // 2, one, 0)

    mine = x // 2
    for c in range(2):
        raw_wait(c)
        parts = combine_quarters(normalize(xin.at[c], toep, box, filt, mag))
        whiten(spectra_of(parts, tab, mine), stage, wsend.at[c], mine)
        section_start(c, mine)
        slot0[pl.ds(8 * x + 4 * c, 4)] = wsend[c, x]
        if c == 1:
            ring_start(1, 1, 0)
            for i in range(NX):
                ring_start(2, 0, i)
        whiten(spectra_of(parts, tab, 1 - mine), stage, wsend.at[c], 1 - mine)
        section_start(c, 1 - mine)
    for i in range(1, NX):
        back_wait(0, i)
    first_start(1)
    for i in range(NX):
        ring_start(2, 1, i)
    near_picks(0)
    near_picks(1)
    near_picks(1 + REACH)
    for h in range(3, REACH + 1):
        for c in range(2):
            for i in range(NX):
                ring_start(h, c, i)
        near_picks(h - 1)
        near_picks(h - 1 + REACH)
    for c in range(2):
        for i in range(NX):
            for d in range(2):
                ring_wait(d, REACH, c, i)
    for k in range(1, REACH + 1):
        far_picks(k)
    near_picks(REACH)
    near_picks(2 * REACH)

    pltpu.make_async_copy(got.at[0:119], got.at[0:119], pr_sem).wait()
    gather_ends(got, ends_s, z, w, left, right, turned)
    tile_products(left, right, turned, mask, valid, made, out_ref, out_sem)

    for b in range(4):
        pltpu.make_async_copy(made.at[b], out_ref.at[b], out_sem.at[b]).wait()
    pltpu.make_async_copy(got.at[0:119], got.at[0:119], ps_sem).wait()
    for c in range(2):
        for i in range(1, NX):
            raw_copy(c, i).wait_send()
            back_copy(c, xpeer(i)).wait_send()
        for i in range(NX):
            for d in range(2):
                if c == 0:
                    first_copy(d, xpeer(i)).wait_send()
                for h in range(1 + (c == 0), REACH + 1):
                    ring_copy(d, h, c, i).wait_send()


def body(raw, taps, pairs, counts):
    ends = pairs.reshape(128, 128, 2).transpose(0, 2, 1).reshape(256, 128)
    any_spec = pl.BlockSpec(memory_space=pl.ANY)
    vmem = pl.BlockSpec(memory_space=pltpu.VMEM)
    dma = pltpu.SemaphoreType.DMA
    tiles = pltpu.VMEM((4, 1536, 128), BF16)
    result = pl.pallas_call(
        whole_kernel,
        out_shape=jax.ShapeDtypeStruct((4, BR, 2, 1536), F32),
        in_specs=[any_spec] * 5,
        out_specs=any_spec,
        scratch_shapes=[
            pltpu.SMEM((33,), F32),
            pltpu.VMEM((256, 128), jnp.int32),
            pltpu.VMEM((1, 128), jnp.int32),
            pltpu.VMEM((4096, 512), F32),
            pltpu.VMEM((2, 4, 1024, 512), BF16),
            pltpu.VMEM((2, NX, CROWS, 1024), BF16),
            pltpu.VMEM((2, 2, 256, 256), BF16),
            pltpu.VMEM((2, 256, 256), BF16),
            pltpu.VMEM((17, CROWS, 256), F32),
            pltpu.VMEM((2, 17, CROWS, 256), BF16),
            pltpu.VMEM((4, 4 * BLK, 128), F32),
            pltpu.VMEM((2, 4, 4, BLK, 128), BF16),
            pltpu.VMEM((16, 128), jnp.int32),
            pltpu.SMEM((16, 128), jnp.int32),
            pltpu.SMEM((16, 128), jnp.int32),
            pltpu.VMEM((9, PLANE, BLK, 128), BF16),
            pltpu.VMEM((2, REACH, PLANE, BLK, 128), BF16),
            pltpu.VMEM((NZ * PLANE, BLK, 128), BF16),
            tiles, tiles, tiles,
            pltpu.VMEM((3, 144, 128), F32),
            pltpu.VMEM((8, 1536), F32),
            pltpu.VMEM((4, BR, 2, 1536), F32),
        ]
        + [pltpu.VMEM((32, BLK, 128), BF16)] * 9
        + [
            dma, dma((2,)), dma((2, 3)), dma((2, 3)), dma((2, 4)), dma((2, 4)),
            dma((2, 4, 8)), dma((2, 4, 8)), dma, dma, dma((5,)), dma((4,)),
        ],
        compiler_params=pltpu.CompilerParams(
            collective_id=0, has_side_effects=True, vmem_limit_bytes=60 << 20
        ),
        name="cross_spectra",
    )(raw, taps, ends, counts.reshape(1, 128), jnp.asarray(dft_tables()))
    return result.transpose(0, 2, 1, 3)


def solution(mesh):
    return jax.shard_map(
        body,
        mesh=mesh,
        in_specs=(P("sta", "sec"), P(), P(), P("sta")),
        out_specs=P("sec", None, None, "sta"),
        check_vma=False,
    )
```
